32 devices in a mesh: req: 8 (over z, y), mlp: 4 (over x, core).
Axes of the slice: x: 2, y: 2, z: 4, core: 2. Of those that a mesh axis runs over, the one named last changes fastest.
Arguments:
- tokens: bfloat16 [2048, 2048], P('req', 'mlp'), may hold values from -5 to 5
- attn_gain: float32 [2048], replicated, may hold values from 0.5 to 1.5
- mlp_gain: float32 [2048], replicated, may hold values from 0.5 to 1.5
- final_gain: float32 [2048], replicated, may hold values from 0.25 to 4
- q_gain: float32 [64], replicated, may hold values from 0.5 to 1.5
- k_gain: float32 [64], replicated, may hold values from 0.25 to 4
- w_query: bfloat16 [2048, 2048], P(None, 'mlp'), may hold values from -0.125 to 0.125
- w_keyval: bfloat16 [2048, 1024], P(None, 'mlp'), may hold values from -0.125 to 0.125
- w_out: bfloat16 [2048, 2048], P('mlp'), may hold values from -0.125 to 0.125
- w_gate: bfloat16 [2048, 8192], P(None, 'mlp'), may hold values from -0.125 to 0.125
- w_up: bfloat16 [2048, 8192], P(None, 'mlp'), may hold values from -0.125 to 0.125
- w_down: bfloat16 [8192, 2048], P('mlp'), may hold values from -0.0625 to 0.0625
- w_head: bfloat16 [2048, 65536], P('req', 'mlp'), may hold values from -0.42 to 0.42
- targets: int32 [2048], P('req'), may hold values from 0 to 65535
- req_lengths: int32 [8, 4], P('req'), may hold values from 1 to 128, 256 in all within a row
- req_tenant: int32 [8, 4], P('req'), may hold values from 0 to 3
- prefix_piece: int32 [8], replicated, may hold values from 0 to 7, each once
- prefix_kv: bfloat16 [8, 2048, 1024], P('req', None, 'mlp'), may hold values from -160 to 160
Outputs:
- hidden_out: bfloat16 [2048, 2048], P('req', 'mlp')
- logprob: float32 [2048], P('req')
The draws below stay inside these ranges and needn't reach their ends.
Inputs may be any that keep to these rules, and one draw needn't show every extreme that they name: `req_lengths`: each row sums to 256; its longest request has exactly 128 tokens. `prefix_piece`: every piece number appears once; piece n is part n % 2 of the prefix of tenant n // 2.
All inputs are finite; a program needn't handle non-finite values.
Results may differ from the reference program's by a relative error of at most 0.023.
Values may be sent and summed in bfloat16 or wider, within the bound.
No kernel may reach another device: no remote copies, remote signals or barrier semaphores. Data moves between devices by JAX's collectives and lax.ppermute only.
A program may use at most 192 MiB of HBM per device.

```python
import math
import jax
import jax.numpy as jnp
import numpy as np
from jax import lax

D = 2048
H = 32
KVH = 8
HD = 64
FF = 8192
VOCAB = 65536
TENANTS = 4
PLEN = 4096
RPG = 4
TOK_GRP = 256
LMOST = 128
PSPLIT = 2
PSLAB = 2048
TOKENS = 2048
N_REQ = 8


def draw_prefix_kv(key, part):
    key_base = jax.random.fold_in(key, 0)
    full_shape = (N_REQ, PSLAB, 2 * HD * KVH)
    return jnp.clip(jax.random.normal(key_base, full_shape, jnp.float32), -4.0, 4.0).astype(jnp.bfloat16)


def draw_tokens(key, part):
    key_base = jax.random.fold_in(key, 1)
    return jnp.clip(jax.random.normal(key_base, (TOKENS, D), jnp.float32), -5.0, 5.0).astype(jnp.bfloat16)


def draw_w_head(key, part):
    key_base = jax.random.fold_in(key, 3)
    return jnp.clip(0.07 * jax.random.normal(key_base, (D, VOCAB), jnp.float32), -0.42, 0.42).astype(jnp.bfloat16)


def plant(result, own_key, low, largest):
    shape = result.shape
    index_at = [jax.random.randint(jax.random.fold_in(own_key, axis), (), 0, shape[axis]) for axis in range(len(shape))]
    result = result.at[tuple(index_at)].set(low)
    longest = shape.index(max(shape))
    index_at[longest] = (index_at[longest] + 1) % shape[longest]
    return result.at[tuple(index_at)].set(largest)


def block_scale(own_key, dims, shards, least, high):
    factor_of, own = 1.0, jax.random.fold_in(own_key, 6)
    for dim, blocks in shards:
        draws = jnp.exp(jax.random.uniform(jax.random.fold_in(own, dim), (blocks,), jnp.float32, least / len(shards), high / len(shards)))
        factor_of = factor_of * jnp.repeat(draws, dims[dim] // blocks).reshape([-1 if axis == dim else 1 for axis in range(len(dims))])
    return factor_of


def profile(count, total, reach, slope):
    portions = [(1 << 20) // math.isqrt(standing ** slope) + 1 for standing in range(2, count + 1)]
    rest, counts = total - reach - (count - 1), [1] * (count - 1)
    while rest > 0:
        candidates = [i for i in range(count - 1) if counts[i] < reach]
        mass, remaining = sum([portions[i] for i in candidates]), rest
        for i in candidates:
            addition = min(reach - counts[i], max(1, remaining * portions[i] // mass), rest)
            counts[i] = counts[i] + addition
            rest = rest - addition
    return np.array([reach] + counts)


def uneven_parts(key, number_of, total, most, lean):
    if number_of == 2:
        one = jax.random.randint(key, (), max(1, total - most), min(most, total - 1) + 1)
        return jnp.stack([one, total - one])
    tallies = jnp.asarray(profile(number_of, total, most, lean), jnp.int32)
    couples = (number_of - 1) // 2
    source_of, taker = tallies[1:1 + 2 * couples:2], tallies[2:2 + 2 * couples:2]
    slack = jnp.minimum(source_of - 1, most - taker)
    moved = jax.random.randint(jax.random.fold_in(key, 1), (couples,), 0, 1 << 20) % (slack + 1)
    tallies = tallies.at[1:1 + 2 * couples:2].set(source_of - moved).at[2:2 + 2 * couples:2].set(taker + moved)
    return tallies[jax.random.permutation(jax.random.fold_in(key, 2), number_of)]


def scatter_about(key, shape, width, bound, cuts=(), kind=jnp.bfloat16):
    level = block_scale(key, shape, cuts, -0.22, 0.18) if cuts else 1.0
    values = jax.random.normal(key, shape, jnp.float32) * width * level
    return jnp.minimum(jnp.maximum(values, -bound), bound).astype(kind)


def setup_inputs(seed: int = 0) -> dict:
    splits = jax.random.split(jax.random.key(seed), 19)
    tokens = draw_tokens(jax.random.fold_in(splits[18], 71), 0)
    attn_gain = jnp.clip(1.0 + 0.1 * jax.random.normal(splits[1], (D,), jnp.float32), 0.5, 1.5)
    mlp_gain = jnp.clip(1.0 + 0.1 * jax.random.normal(splits[2], (D,), jnp.float32), 0.5, 1.5)
    final_gain = jnp.clip(jnp.exp(jax.random.uniform(splits[3], (D,), jnp.float32, math.log(0.25), math.log(4.0))), 0.25, 4.0)
    q_gain = jnp.clip(1.0 + 0.1 * jax.random.normal(splits[4], (HD,), jnp.float32), 0.5, 1.5)
    k_gain = jnp.clip(jnp.exp(jax.random.uniform(splits[5], (HD,), jnp.float32, math.log(0.25), math.log(4.0))), 0.25, 4.0)
    w_query = scatter_about(splits[6], (D, H * HD), D ** -0.5, 0.125, ((1, 4),))
    w_keyval = scatter_about(splits[7], (D, KVH * 2 * HD), D ** -0.5, 0.125, ((1, 4),))
    w_out = scatter_about(splits[8], (H * HD, D), (H * HD) ** -0.5, 0.125, ((0, 4),))
    w_gate = scatter_about(splits[9], (D, FF), D ** -0.5, 0.125, ((1, 4),))
    w_up = scatter_about(splits[10], (D, FF), D ** -0.5, 0.125, ((1, 4),))
    w_down = scatter_about(splits[11], (FF, D), FF ** -0.5, 0.0625, ((0, 4),))
    w_head = draw_w_head(jax.random.fold_in(splits[18], 71), 0)
    targets = plant(jax.random.randint(splits[13], (TOKENS,), 0, VOCAB), jax.random.fold_in(splits[13], 1), 0, VOCAB - 1).astype(jnp.int32)
    req_lengths = jax.vmap(lambda own: uneven_parts(own, RPG, TOK_GRP, LMOST, 2))(jax.random.split(splits[14], N_REQ)).reshape((N_REQ, RPG)).astype(jnp.int32)
    req_tenant = plant(jax.random.randint(splits[15], (N_REQ, RPG), 0, TENANTS), jax.random.fold_in(splits[15], 1), 0, TENANTS - 1).astype(jnp.int32)
    prefix_piece = jax.random.permutation(splits[16], N_REQ).astype(jnp.int32)
    prefix_kv = draw_prefix_kv(jax.random.fold_in(splits[18], 71), 0)
    return dict(tokens=tokens, attn_gain=attn_gain, mlp_gain=mlp_gain, final_gain=final_gain, q_gain=q_gain, k_gain=k_gain, w_query=w_query, w_keyval=w_keyval, w_out=w_out, w_gate=w_gate, w_up=w_up, w_down=w_down, w_head=w_head, targets=targets, req_lengths=req_lengths, req_tenant=req_tenant, prefix_piece=prefix_piece, prefix_kv=prefix_kv)


EPS = 1e-05
LOG_THETA = math.log(1000000.0)
NEG = -1e+30

def rms_norm(values, gain):
    return values * lax.rsqrt(lax.optimization_barrier(jnp.mean(values * values, axis=-1, keepdims=True)) + EPS) * gain

def rope_tables(position, size):
    half = size // 2
    freq = jnp.exp(jnp.arange(half, dtype=jnp.float32) * (-2.0 * LOG_THETA / size))
    angle = position[:, None] * freq[None, :]
    return (jnp.cos(angle), jnp.sin(angle))

def rotate(values, cosine, sine):
    half = values.shape[-1] // 2
    first = values[..., :half]
    second = values[..., half:]
    cosine = cosine[:, None, :]
    sine = sine[:, None, :]
    return jnp.concatenate([first * cosine - second * sine, first * sine + second * cosine], axis=-1)

def row_layout(lengths, tenants, count):
    ends = jnp.cumsum(lengths).astype(jnp.int32)
    row_ids = jnp.arange(count, dtype=jnp.int32)
    request = lax.optimization_barrier(jnp.sum((row_ids[:, None] >= ends[None, :]).astype(jnp.int32), axis=1)).astype(jnp.int32)
    onehot = (request[:, None] == jnp.arange(lengths.shape[0], dtype=jnp.int32)[None, :]).astype(jnp.int32)
    starts = (ends - lengths).astype(jnp.int32)
    offset = (row_ids - lax.optimization_barrier(jnp.sum(onehot * starts[None, :], axis=1))).astype(jnp.int32)
    tenant = lax.optimization_barrier(jnp.sum(onehot * tenants[None, :], axis=1)).astype(jnp.int32)
    return (request, offset, tenant)

def reference(tokens, attn_gain, mlp_gain, final_gain, q_gain, k_gain, w_query, w_keyval, w_out, w_gate, w_up, w_down, w_head, targets, req_lengths, req_tenant, prefix_piece, prefix_kv):
    group = H // KVH
    scale = HD ** (-0.5)
    prefix = prefix_kv.reshape(N_REQ * PSLAB, KVH, 2, HD)
    pre_keys = prefix[:, :, 0].transpose(1, 0, 2)
    pre_vals = prefix[:, :, 1].transpose(1, 0, 2)
    key_tenant = jnp.repeat((prefix_piece // PSPLIT).astype(jnp.int32), PSLAB)

    def one_group(index):
        stream = lax.dynamic_slice_in_dim(tokens, (index * TOK_GRP).astype(jnp.int32), TOK_GRP, 0)
        lengths = lax.dynamic_index_in_dim(req_lengths, index, 0, keepdims=False)
        tenants = lax.dynamic_index_in_dim(req_tenant, index, 0, keepdims=False)
        wanted = lax.dynamic_slice_in_dim(targets, (index * TOK_GRP).astype(jnp.int32), TOK_GRP, 0)
        stream_f = stream.astype(jnp.float32)
        normed = rms_norm(stream_f, attn_gain).astype(jnp.bfloat16)
        query = jnp.dot(normed, w_query, preferred_element_type=jnp.float32).reshape(TOK_GRP, H, HD)
        keyval = jnp.dot(normed, w_keyval, preferred_element_type=jnp.float32).reshape(TOK_GRP, KVH, 2, HD)
        request, offset, tenant = row_layout(lengths, tenants, TOK_GRP)
        cosine, sine = rope_tables((PLEN + offset).astype(jnp.float32), HD)
        query = rotate(rms_norm(query, q_gain), cosine, sine).astype(jnp.bfloat16)
        own_keys = rotate(rms_norm(keyval[:, :, 0], k_gain), cosine, sine).astype(jnp.bfloat16).transpose(1, 0, 2)
        own_vals = keyval[:, :, 1].astype(jnp.bfloat16).transpose(1, 0, 2)
        queries = query.reshape(TOK_GRP, KVH, group, HD).transpose(1, 2, 0, 3).reshape(KVH, group * TOK_GRP, HD)
        row_ids = jnp.arange(TOK_GRP, dtype=jnp.int32)
        causal = (request[:, None] == request[None, :]) & (row_ids[None, :] <= row_ids[:, None])
        seen_prefix = tenant[:, None] == key_tenant[None, :]
        seen = jnp.tile(jnp.concatenate([seen_prefix, causal], axis=1), (group, 1))

        def one_head(kv_index):
            qhead = lax.dynamic_index_in_dim(queries, kv_index, 0, keepdims=False)
            keys = jnp.concatenate([lax.dynamic_index_in_dim(pre_keys, kv_index, 0, keepdims=False), lax.dynamic_index_in_dim(own_keys, kv_index, 0, keepdims=False)], axis=0)
            vals = jnp.concatenate([lax.dynamic_index_in_dim(pre_vals, kv_index, 0, keepdims=False), lax.dynamic_index_in_dim(own_vals, kv_index, 0, keepdims=False)], axis=0)
            scores = jnp.dot(qhead, keys.T, preferred_element_type=jnp.float32) * scale
            scores = jnp.where(seen, scores, NEG)
            top = lax.optimization_barrier(jnp.max(scores, axis=1, keepdims=True))
            weights = jnp.where(seen, jnp.exp(scores - top), 0.0)
            total = lax.optimization_barrier(jnp.sum(weights, axis=1, keepdims=True))
            accum = jnp.dot(weights.astype(jnp.bfloat16), vals, preferred_element_type=jnp.float32)
            return accum / total
        heads = lax.map(one_head, jnp.arange(KVH, dtype=jnp.int32))
        attended = heads.reshape(KVH, group, TOK_GRP, HD).transpose(2, 0, 1, 3).reshape(TOK_GRP, H * HD).astype(jnp.bfloat16)
        mid = (stream_f + jnp.dot(attended, w_out, preferred_element_type=jnp.float32)).astype(jnp.bfloat16)
        mid_f = mid.astype(jnp.float32)
        normed_mid = rms_norm(mid_f, mlp_gain).astype(jnp.bfloat16)
        gate = jnp.dot(normed_mid, w_gate, preferred_element_type=jnp.float32)
        upper = jnp.dot(normed_mid, w_up, preferred_element_type=jnp.float32)
        inner = (jax.nn.silu(gate) * upper).astype(jnp.bfloat16)
        hidden = (mid_f + jnp.dot(inner, w_down, preferred_element_type=jnp.float32)).astype(jnp.bfloat16)
        normed_out = rms_norm(hidden.astype(jnp.float32), final_gain).astype(jnp.bfloat16)
        logits = jnp.dot(normed_out, w_head, preferred_element_type=jnp.float32)
        top = lax.optimization_barrier(jnp.max(logits, axis=1))
        total = lax.optimization_barrier(jnp.sum(jnp.exp(logits - top[:, None]), axis=1))
        picked = jnp.take_along_axis(logits, wanted[:, None].astype(jnp.int32), axis=1)[:, 0]
        return (hidden, picked - top - jnp.log(total))
    hidden_all, logprob_all = lax.map(one_group, jnp.arange(N_REQ, dtype=jnp.int32))
    return (hidden_all.reshape(TOKENS, D), logprob_all.reshape(TOKENS))
```

```python
import functools
import math

import jax
import jax.numpy as jnp
from jax import lax
from jax.experimental import pallas as pl
from jax.experimental.pallas import tpu as pltpu
from jax.sharding import PartitionSpec as P

TENANTS = 4
PLEN = 4096

EPS = 1e-05
LOG_THETA = math.log(1000000.0)
NEG = -1e30
BF = jnp.bfloat16
F32 = jnp.float32
LANES = 128
BLOCK = 64
KEYS = 1024
MIB = 1 << 20


def params(mib, **more):
    return pltpu.CompilerParams(vmem_limit_bytes=mib * MIB, **more)


def swap(values, axis, bit):
    size = lax.axis_size(axis)
    return lax.ppermute(values, axis, [(i, i ^ bit) for i in range(size)])


def after(values, *events):
    return lax.optimization_barrier((values, *events))[0]


def bits_of(size):
    found = []
    while size > 1:
        size //= 2
        found.append(size)
    return found


def row_layout(lengths, tenants, count):
    ends = jnp.cumsum(lengths)
    row_ids = jnp.arange(count, dtype=jnp.int32)
    request = jnp.sum((row_ids[:, None] >= ends[None, :]).astype(jnp.int32), axis=1)
    onehot = (request[:, None] == jnp.arange(lengths.shape[0], dtype=jnp.int32)[None, :]).astype(
        jnp.int32
    )
    starts = ends - lengths
    offset = row_ids - jnp.sum(onehot * starts[None, :], axis=1)
    tenant = jnp.sum(onehot * tenants[None, :], axis=1)
    return (request, offset, tenant)


def rope_tables(position, size):
    half = size // 2
    freq = jnp.exp(jnp.arange(half, dtype=jnp.float32) * (-2.0 * LOG_THETA / size))
    angle = position[:, None] * freq[None, :]
    cosine, sine = jnp.cos(angle), jnp.sin(angle)
    wide = LANES // size
    return (
        jnp.tile(jnp.concatenate([cosine, cosine], axis=1), (1, wide)),
        jnp.tile(jnp.concatenate([-sine, sine], axis=1), (1, wide)),
    )


def lane_ids(shape):
    return lax.broadcasted_iota(jnp.int32, shape, len(shape) - 1)


def qkv_kernel(place, *refs, width, pieces, scale):
    stream = refs[:pieces]
    gain, wq, wkv, cosine, sine, q_gain, k_gain, q_out, key_out, value_out = refs[pieces:]
    me = place[0]
    model = width * pieces
    loaded = [part[...].astype(F32) for part in stream]
    squares = sum(jnp.sum(part * part, axis=-1, keepdims=True) for part in loaded)
    factor = lax.rsqrt(squares / model + EPS)
    query = None
    keyval = None
    for j in range(pieces):
        quarter = me ^ j
        normed = (loaded[j] * factor * gain[pl.ds(quarter, 1), :]).astype(BF)
        rows = pl.ds(pl.multiple_of(quarter * width, width), width)
        q_part = jnp.dot(normed, wq[rows, :], preferred_element_type=F32)
        kv_part = jnp.dot(normed, wkv[rows, :], preferred_element_type=F32)
        query = q_part if query is None else query + q_part
        keyval = kv_part if keyval is None else keyval + kv_part
    lane = lane_ids((query.shape[0], LANES))
    low = lane < 64
    first = (lane % 64) < 32
    cos_t, sin_t = cosine[...], sine[...]

    def roped(tile, factor_of, head_gain):
        value = tile * factor_of * head_gain
        turned = jnp.where(
            first, pltpu.roll(value, LANES - 32, 1), pltpu.roll(value, 32, 1)
        )
        return value * cos_t + turned * sin_t

    for t in range(query.shape[1] // LANES):
        tile = query[:, t * LANES : (t + 1) * LANES]
        square = tile * tile
        one = jnp.sum(jnp.where(low, square, 0.0), axis=-1, keepdims=True)
        two = jnp.sum(jnp.where(low, 0.0, square), axis=-1, keepdims=True)
        factor_of = lax.rsqrt(jnp.where(low, one, two) / 64.0 + EPS)
        result = roped(tile, factor_of, q_gain[...]).astype(BF)
        q_out[:, t * LANES : (t + 1) * LANES] = (result.astype(F32) * scale).astype(BF)
    heads = keyval.shape[1] // LANES
    keys, values = [], []
    for t in range(heads):
        tile = keyval[:, t * LANES : (t + 1) * LANES]
        one = jnp.sum(jnp.where(low, tile * tile, 0.0), axis=-1, keepdims=True)
        factor_of = lax.rsqrt(one / 64.0 + EPS)
        keys.append(roped(tile, factor_of, k_gain[...]))
        values.append(tile)
    for t in range(0, heads, 2):
        wide = slice(t * 64, min(t + 2, heads) * 64)
        key, value = keys[t], pltpu.roll(values[t], 64, 1)
        if t + 1 < heads:
            key = jnp.where(low, key, pltpu.roll(keys[t + 1], 64, 1))
            value = jnp.where(low, value, values[t + 1])
        count = wide.stop - wide.start
        key_out[:, wide] = key[:, :count].astype(BF)
        value_out[wide, :] = jnp.transpose(value)[:count].astype(BF)


def qkv_call(place, stream, gain, wq, wkv, cosine, sine, q_gain, k_gain):
    pieces = len(stream)
    rows, width = stream[0].shape
    head = q_gain.shape[0]
    twice = LANES // head
    kernel = functools.partial(qkv_kernel, width=width, pieces=pieces, scale=head**-0.5)
    whole = pl.BlockSpec(memory_space=pltpu.VMEM)
    return pl.pallas_call(
        kernel,
        out_shape=(
            jax.ShapeDtypeStruct((rows, wq.shape[1]), BF),
            jax.ShapeDtypeStruct((rows, wkv.shape[1] // 2), BF),
            jax.ShapeDtypeStruct((wkv.shape[1] // 2, rows), BF),
        ),
        in_specs=[pl.BlockSpec(memory_space=pltpu.SMEM)] + [whole] * (pieces + 7),
        out_specs=(whole, whole, whole),
        compiler_params=params(24),
        cost_estimate=pl.CostEstimate(
            flops=2 * rows * width * pieces * (wq.shape[1] + wkv.shape[1]),
            bytes_accessed=2 * (wq.size + wkv.size + rows * width * pieces),
            transcendentals=0,
        ),
        name="qkv",
    )(
        place,
        *stream,
        gain.reshape(pieces, width),
        wq,
        wkv,
        cosine,
        sine,
        jnp.tile(q_gain, twice).reshape(1, LANES),
        jnp.tile(k_gain, twice).reshape(1, LANES),
    )


def split_kernel(kv, key_out, value_out, *, heads):
    low = lane_ids((kv.shape[0], LANES)) < 64
    for t in range(0, heads, 2):
        wide = slice(t * 64, min(t + 2, heads) * 64)
        count = wide.stop - wide.start
        first = kv[:, t * LANES : (t + 1) * LANES].astype(F32)
        key, value = first, pltpu.roll(first, 64, 1)
        if t + 1 < heads:
            second = kv[:, (t + 1) * LANES : (t + 2) * LANES].astype(F32)
            key = jnp.where(low, key, pltpu.roll(second, 64, 1))
            value = jnp.where(low, value, second)
        key_out[:, wide] = key[:, :count].astype(BF)
        value_out[wide, :] = jnp.transpose(value)[:count].astype(BF)


def split_call(kv):
    slab, wide = kv.shape
    rows = 256
    return pl.pallas_call(
        functools.partial(split_kernel, heads=wide // LANES),
        out_shape=(
            jax.ShapeDtypeStruct((slab, wide // 2), BF),
            jax.ShapeDtypeStruct((wide // 2, slab), BF),
        ),
        grid=(slab // rows,),
        in_specs=[pl.BlockSpec((rows, wide), lambda i: (i, 0))],
        out_specs=(
            pl.BlockSpec((rows, wide // 2), lambda i: (i, 0)),
            pl.BlockSpec((wide // 2, rows), lambda i: (0, i)),
        ),
        compiler_params=params(16),
        cost_estimate=pl.CostEstimate(flops=0, bytes_accessed=4 * kv.size, transcendentals=0),
        name="split",
    )(kv)


def attention_kernel(flags, owners, *refs, pieces, heads, group, own, slab):
    q_ref, tenant_ref, kv_refs, rest = refs[0], refs[1], refs[2 : 2 + 2 * pieces], refs[2 + 2 * pieces :]
    if own:
        own_key, own_value, begin_ref = rest[:3]
        rest = rest[3:]
    out, lse_out, qp, best, total, accum = rest
    block = pl.program_id(0)
    count = heads * group
    wide = heads * 64
    low = lane_ids((BLOCK, LANES)) < 64

    for i in range(count):
        tile = q_ref[:, (i // 2) * LANES : (i // 2 + 1) * LANES].astype(F32)
        place = (i // group) % 2
        if i % 2 != place:
            tile = pltpu.roll(tile, 64, 1)
        tile = jnp.where(low if place == 0 else ~low, tile, 0.0).astype(BF)
        rows = slice(i * BLOCK, (i + 1) * BLOCK)
        for t in range(0, wide, LANES):
            here = min(LANES, wide - t)
            mine = t // LANES == i // group // 2
            qp[rows, t : t + here] = tile[:, :here] if mine else jnp.zeros((BLOCK, here), BF)

    tenants = tenant_ref[0]

    def attend(keys, values, span, mask=None):
        found = None
        for c in range(0, span, min(KEYS, span)):
            part = slice(c, c + min(KEYS, span))
            score = lax.dot_general(
                keys[part, :], qp[...], (((1,), (1,)), ((), ())), preferred_element_type=F32
            )
            if mask is not None:
                score = jnp.where(mask, score, NEG)
            top = jnp.max(score, axis=0, keepdims=True)
            if found is not None:
                top = jnp.maximum(top, found[0])
            weight = jnp.exp(score - top)
            if mask is not None:
                weight = jnp.where(mask, weight, 0.0)
            summed = jnp.sum(weight, axis=0, keepdims=True)
            value = jnp.dot(values[:, part], weight.astype(BF), preferred_element_type=F32)
            if found is not None:
                keep = jnp.exp(found[0] - top)
                summed = found[1] * keep + summed
                value = found[2] * keep + value
            found = (top, summed, value)
        return found

    if own:
        span = own_key.shape[0]
        key_id = lax.broadcasted_iota(jnp.int32, (span, count * BLOCK), 0)
        row_id = block * BLOCK + lane_ids((1, count * BLOCK)) % BLOCK
        seen = (key_id <= row_id) & (key_id >= begin_ref[0])
        best[...], total[...], accum[...] = attend(own_key, own_value, span, seen)
    else:
        best[...] = jnp.full(best.shape, NEG, F32)
        total[...] = jnp.zeros(total.shape, F32)
        accum[...] = jnp.zeros(accum.shape, F32)

    for j in range(pieces):

        @pl.when(flags[block, j] > 0)
        def _(j=j):
            top, summed, value = attend(kv_refs[2 * j], kv_refs[2 * j + 1], slab)
            ok = tenants == owners[j]
            old = best[...]
            new = jnp.where(ok, jnp.maximum(old, top), old)
            keep = jnp.where(ok, jnp.exp(old - new), 1.0)
            add = jnp.where(ok, jnp.exp(jnp.where(ok, top - new, 0.0)), 0.0)
            best[...] = new
            total[...] = total[...] * keep + summed * add
            accum[...] = accum[...] * keep + value * add

    row_total = total[...]
    some = row_total > 0.0
    safe = jnp.where(some, row_total, 1.0)
    lse = jnp.where(some, best[...] + jnp.log(safe), NEG)
    inverse = 1.0 / safe
    lane = lane_ids((1, count * BLOCK))
    result = accum[:64, :]
    for h in range(1, heads):
        result = jnp.where(lane < h * group * BLOCK, result, accum[h * 64 : (h + 1) * 64, :])
    result = result * inverse
    if own:
        out[0] = result
        lse_out[0] = lse
    else:
        high = lse.astype(BF).astype(F32)
        middle = (lse - high).astype(BF).astype(F32)
        last = (lse - high - middle).astype(BF).astype(F32)
        line = lax.broadcasted_iota(jnp.int32, (16, count * BLOCK), 0)
        packed = jnp.where(
            line == 0, high, jnp.where(line == 1, middle, jnp.where(line == 2, last, 0.0))
        )
        out[0, :64, :] = result.astype(BF)
        out[0, 64:, :] = packed.astype(BF)
        lse_out[0] = lse


def attention_call(query, tenant, flags, owners, pieces, own_part):
    rows, width = query.shape
    slab, wide = pieces[0][0].shape
    own = own_part is not None
    heads = wide // 64
    group = width // 64 // heads
    stack = heads * group * BLOCK
    blocks = rows // BLOCK
    full = lambda array: pl.BlockSpec(array.shape, lambda b, *_: (0, 0))
    lanes = pl.BlockSpec((1, 1, stack), lambda b, *_: (b, 0, 0))
    operands = [query, tenant] + [array for piece in pieces for array in piece]
    in_specs = [pl.BlockSpec((BLOCK, width), lambda b, *_: (b, 0)), lanes]
    in_specs += [full(array) for piece in pieces for array in piece]
    if own:
        own_key, own_value, begin = own_part
        operands += [own_key, own_value, begin]
        in_specs += [full(own_key), full(own_value), lanes]
    depth = 64 if own else 80
    kernel = functools.partial(
        attention_kernel, pieces=len(pieces), heads=heads, group=group, own=own, slab=slab
    )
    return pl.pallas_call(
        kernel,
        out_shape=(
            jax.ShapeDtypeStruct((blocks, depth, stack), F32 if own else BF),
            jax.ShapeDtypeStruct((blocks, 1, stack), F32),
        ),
        grid_spec=pltpu.PrefetchScalarGridSpec(
            num_scalar_prefetch=2,
            grid=(blocks,),
            in_specs=in_specs,
            out_specs=(pl.BlockSpec((1, depth, stack), lambda b, *_: (b, 0, 0)), lanes),
            scratch_shapes=[
                pltpu.VMEM((stack, wide), BF),
                pltpu.VMEM((1, stack), F32),
                pltpu.VMEM((1, stack), F32),
                pltpu.VMEM((wide, stack), F32),
            ],
        ),
        compiler_params=params(40),
        cost_estimate=pl.CostEstimate(
            flops=4 * rows * group * slab * wide * 4,
            bytes_accessed=4 * slab * wide * len(pieces),
            transcendentals=rows * group * heads * slab,
        ),
        name="attention_own" if own else "attention_partner",
    )(flags, owners, *operands)


def project_kernel(
    place, one, lse_one, two, w_out, kept, sent, attended, *, count, width, pieces
):
    me = place[0]
    for b in range(one.shape[0]):
        first = lse_one[b]
        extra = two[b, 64:, :].astype(F32)
        second = extra[0:1] + extra[1:2] + extra[2:3]
        share_one = 1.0 / (1.0 + jnp.exp(second - first))
        share_two = 1.0 / (1.0 + jnp.exp(first - second))
        merged = one[b] * share_one + two[b, :64, :].astype(F32) * share_two
        rows = jnp.transpose(jnp.concatenate([merged, jnp.zeros_like(merged)], axis=0))
        for t in range(count // 2):
            left = rows[2 * t * BLOCK : (2 * t + 1) * BLOCK]
            right = rows[(2 * t + 1) * BLOCK : (2 * t + 2) * BLOCK]
            attended[b * BLOCK : (b + 1) * BLOCK, t * LANES : (t + 1) * LANES] = (
                left + pltpu.roll(right, 64, 1)
            ).astype(BF)
    for j in range(pieces):
        columns = pl.ds(pl.multiple_of((me ^ j) * width, width), width)
        part = jnp.dot(attended[...], w_out[:, columns], preferred_element_type=F32)
        (sent if j % 2 else kept)[j // 2] = part.astype(BF)


def project_call(place, one, lse_one, two, w_out, pieces):
    rows = one.shape[0] * BLOCK
    model = w_out.shape[1]
    width = model // pieces
    whole = pl.BlockSpec(memory_space=pltpu.VMEM)
    half = jax.ShapeDtypeStruct((pieces // 2, rows, width), BF)
    kernel = functools.partial(
        project_kernel, count=w_out.shape[0] // 64, width=width, pieces=pieces
    )
    return pl.pallas_call(
        kernel,
        out_shape=(half, half),
        in_specs=[pl.BlockSpec(memory_space=pltpu.SMEM)] + [whole] * 4,
        out_specs=(whole, whole),
        scratch_shapes=[pltpu.VMEM((rows, w_out.shape[0]), BF)],
        compiler_params=params(24),
        cost_estimate=pl.CostEstimate(
            flops=2 * rows * w_out.size, bytes_accessed=2 * w_out.size, transcendentals=0
        ),
        name="project",
    )(place, one, lse_one, two, w_out)


def swiglu_kernel(
    place, ours, theirs, gain, w_gate, w_up, w_down, kept, sent, normed, accum, *, pieces, width
):
    step = pl.program_id(0)
    me = place[0]

    @pl.when(step == 0)
    def _():
        loaded = [
            (theirs if j % 2 else ours)[j // 2].astype(F32) for j in range(pieces)
        ]
        squares = sum(jnp.sum(part * part, axis=-1, keepdims=True) for part in loaded)
        factor = lax.rsqrt(squares / (pieces * width) + EPS)
        for j in range(pieces):
            quarter = me ^ j
            columns = pl.ds(pl.multiple_of(quarter * width, width), width)
            normed[:, columns] = (loaded[j] * factor * gain[pl.ds(quarter, 1), :]).astype(BF)
        accum[...] = jnp.zeros_like(accum)

    gate = jnp.dot(normed[...], w_gate[...], preferred_element_type=F32)
    upper = jnp.dot(normed[...], w_up[...], preferred_element_type=F32)
    inner = (gate / (1.0 + jnp.exp(-gate)) * upper).astype(BF)
    accum[...] += jnp.dot(inner, w_down[...], preferred_element_type=F32)

    @pl.when(step == pl.num_programs(0) - 1)
    def _():
        for j in range(pieces):
            columns = pl.ds(pl.multiple_of((me ^ j) * width, width), width)
            (sent if j % 2 else kept)[j // 2] = accum[:, columns].astype(BF)


def swiglu_call(place, ours, theirs, gain, w_gate, w_up, w_down):
    half_pieces, rows, width = ours.shape
    pieces = 2 * half_pieces
    model, units = w_gate.shape
    tile = 256
    whole = pl.BlockSpec((half_pieces, rows, width), lambda s, *_: (0, 0, 0))
    half = jax.ShapeDtypeStruct((half_pieces, rows, width), BF)
    kernel = functools.partial(swiglu_kernel, pieces=pieces, width=width)
    return pl.pallas_call(
        kernel,
        out_shape=(half, half),
        grid_spec=pltpu.PrefetchScalarGridSpec(
            num_scalar_prefetch=1,
            grid=(units // tile,),
            in_specs=[
                whole,
                whole,
                pl.BlockSpec((pieces, width), lambda s, *_: (0, 0)),
                pl.BlockSpec((model, tile), lambda s, *_: (0, s)),
                pl.BlockSpec((model, tile), lambda s, *_: (0, s)),
                pl.BlockSpec((tile, model), lambda s, *_: (s, 0)),
            ],
            out_specs=(whole, whole),
            scratch_shapes=[
                pltpu.VMEM((rows, model), BF),
                pltpu.VMEM((rows, model), F32),
            ],
        ),
        compiler_params=params(40),
        cost_estimate=pl.CostEstimate(
            flops=6 * rows * model * units,
            bytes_accessed=6 * model * units,
            transcendentals=rows * units,
        ),
        name="swiglu",
    )(place, ours, theirs, gain.reshape(pieces, width), w_gate, w_up, w_down)


def head_kernel(place, *refs, depth, offset, span, width, pieces, blocks, cuts, step_cols):
    quads = refs[:4]
    gain, targets = refs[4:6]
    count = blocks * cuts
    w_refs = refs[6 : 6 + count]
    out, w_full, normed, sems = refs[6 + count :]
    me_req, me_mlp = place[1], place[0]
    step = pl.program_id(0)
    columns_here = w_full.shape[1]
    cut = columns_here // cuts

    @pl.when(step == 0)
    def _():
        copies = [
            pltpu.make_async_copy(
                w_refs[n].at[:depth, :],
                w_full.at[
                    pl.ds(pl.multiple_of((me_req ^ (n % blocks)) * depth, depth), depth),
                    pl.ds(n // blocks * cut, cut),
                ],
                sems.at[n],
            )
            for n in range(count)
        ]
        for copy in copies:
            copy.start()
        for copy in copies:
            copy.wait()

    rows_half = quads[0].shape[-2]
    for part in range(2):
        own_ref, other_ref = quads[2 * part], quads[2 * part + 1]
        loaded = []
        for j in range(pieces):
            source = (other_ref if j % 2 else own_ref)[...].reshape(
                pieces // 2, rows_half, width
            )
            loaded.append(source[j // 2].astype(F32))
        squares = sum(jnp.sum(value * value, axis=-1, keepdims=True) for value in loaded)
        factor = lax.rsqrt(squares / (pieces * width) + EPS)
        for j in range(pieces):
            quarter = me_mlp ^ j
            where = pl.ds(pl.multiple_of(quarter * width, width), width)
            normed[part * rows_half : (part + 1) * rows_half, where] = (
                loaded[j] * factor * gain[pl.ds(quarter, 1), :]
            ).astype(BF)

    rows = 2 * rows_half
    lane = lane_ids((rows, LANES))
    base = me_mlp * (span * blocks) + me_req * span + offset
    wanted = targets[...] - base
    best = jnp.full((rows, LANES), NEG, F32)
    total = jnp.zeros((rows, LANES), F32)
    picked = jnp.zeros((rows, LANES), F32)
    for c in range(columns_here // step_cols):
        logits = jnp.dot(
            normed[...],
            w_full[:, c * step_cols : (c + 1) * step_cols],
            preferred_element_type=F32,
        )
        tiles = [logits[:, t * LANES : (t + 1) * LANES] for t in range(step_cols // LANES)]
        new = functools.reduce(jnp.maximum, tiles, best)
        total = total * jnp.exp(best - new)
        for t, tile in enumerate(tiles):
            total = total + jnp.exp(tile - new)
            hit = lane == wanted - (c * step_cols + t * LANES)
            picked = picked + jnp.where(hit, tile, 0.0)
        best = new
    top = jnp.max(best, axis=-1, keepdims=True)
    summed = jnp.sum(total * jnp.exp(best - top), axis=-1, keepdims=True)
    chosen = jnp.sum(picked, axis=-1, keepdims=True)
    joined = jnp.where(lane == 0, top, jnp.where(lane == 1, summed, chosen))
    out[...] = jnp.transpose(joined)[:8][None]


def head_call(place, quads, gain, targets, w_parts, depth, offset, span):
    blocks = len(w_parts[0])
    cut = w_parts[0][0].shape[1]
    columns = cut * len(w_parts)
    half_rows, width = quads[0][0].shape[-2:]
    model = depth * blocks
    pieces = model // width
    rows = 2 * half_rows

    def spec(order):
        def index(s, place_ref):
            where = {"y": s % 2, "z": s // 2, "x": 0}
            return tuple(where[name] for name in order) + (0, 0)

        shape = tuple(pieces // 2 if name == "x" else 1 for name in order)
        return pl.BlockSpec(shape + (half_rows, width), index)

    step_cols = min(512, columns)
    kernel = functools.partial(
        head_kernel,
        depth=depth,
        offset=offset,
        span=span,
        width=width,
        pieces=pieces,
        blocks=blocks,
        cuts=len(w_parts),
        step_cols=step_cols,
    )
    return pl.pallas_call(
        kernel,
        out_shape=jax.ShapeDtypeStruct((blocks, 8, rows), F32),
        grid_spec=pltpu.PrefetchScalarGridSpec(
            num_scalar_prefetch=1,
            grid=(blocks,),
            in_specs=[spec(order) for _, order in quads]
            + [
                pl.BlockSpec((pieces, width), lambda s, place_ref: (0, 0)),
                pl.BlockSpec((rows, 1), lambda s, place_ref: (s, 0)),
            ]
            + [pl.BlockSpec(memory_space=pl.ANY)] * (blocks * len(w_parts)),
            out_specs=pl.BlockSpec((1, 8, rows), lambda s, place_ref: (s ^ place_ref[1], 0, 0)),
            scratch_shapes=[
                pltpu.VMEM((model, columns), BF),
                pltpu.VMEM((rows, model), BF),
                pltpu.SemaphoreType.DMA((blocks * len(w_parts),)),
            ],
        ),
        compiler_params=params(40),
        cost_estimate=pl.CostEstimate(
            flops=2 * rows * blocks * model * columns,
            bytes_accessed=2 * model * columns + 2 * rows * blocks * model,
            transcendentals=rows * blocks * columns,
        ),
        name="head",
    )(place, *[array for array, _ in quads], gain.reshape(pieces, width), targets, *sum(w_parts, []))


def merge_stats(one, two):
    top = jnp.maximum(one[..., 0, :], two[..., 0, :])
    total = one[..., 1, :] * jnp.exp(one[..., 0, :] - top) + two[..., 1, :] * jnp.exp(
        two[..., 0, :] - top
    )
    return jnp.stack([top, total, one[..., 2, :] + two[..., 2, :]], axis=-2)


def body(
    tokens,
    attn_gain,
    mlp_gain,
    final_gain,
    q_gain,
    k_gain,
    w_query,
    w_keyval,
    w_out,
    w_gate,
    w_up,
    w_down,
    w_head,
    targets,
    req_lengths,
    req_tenant,
    prefix_piece,
    prefix_kv,
):
    rows, width = tokens.shape
    groups = lax.axis_size("req")
    parts = lax.axis_size("mlp")
    half = groups // 2
    me_req = lax.axis_index("req")
    me_mlp = lax.axis_index("mlp")
    place = jnp.stack([me_mlp, me_req]).astype(jnp.int32)
    split_count = groups // TENANTS
    head_size = q_gain.shape[0]

    meta = jnp.concatenate([req_lengths, req_tenant], axis=1)
    meta_far = swap(meta, "req", half)
    per = req_lengths.shape[1]

    span = w_head.shape[1] // groups
    parts_of_span = 4
    cut = span // parts_of_span
    coded = jnp.concatenate([targets >> 8, targets & 255]).astype(F32).astype(BF)
    coded = coded.reshape(-1, cut)
    extra = jnp.pad(coded, ((0, 16 - coded.shape[0]), (0, 0)))

    def head_part(part, k):
        block = lax.dynamic_slice_in_dim(w_head, (me_req ^ k) * span + part * cut, cut, 1)
        return jnp.concatenate([block, extra], axis=0) if part == 0 else block

    own_parts = [head_part(part, 0) for part in range(parts_of_span)]
    out_parts = [[head_part(part, k) for k in range(1, groups)] for part in range(parts_of_span)]

    def send_part(part, event):
        blocks = after(tuple(out_parts[part]), event)
        return [own_parts[part]] + [
            swap(block, "req", k) for k, block in zip(range(1, groups), blocks)
        ]

    stream = [tokens]
    for bit in [b for b in bits_of(parts) if b > 1][::-1]:
        got = swap(jnp.concatenate(stream, axis=1), "mlp", bit)
        stream = stream + [got[:, i * width : (i + 1) * width] for i in range(len(stream))]
    got = swap(jnp.concatenate(stream, axis=1), "mlp", 1)
    stream = [
        part
        for i, mine in enumerate(stream)
        for part in (mine, got[:, i * width : (i + 1) * width])
    ]

    stream, own_parts, out_parts = lax.optimization_barrier((stream, own_parts, out_parts))

    pieces = [split_call(prefix_kv[0])]
    for k in range(1, half):
        least, most = k & -k, 1 << (k.bit_length() - 1)
        pieces.append(
            (swap(pieces[k ^ least][0], "req", least), swap(pieces[k ^ most][1], "req", most))
        )

    request, offset, tenant = row_layout(req_lengths[0], req_tenant[0], rows)
    _, _, tenant_far = row_layout(meta_far[0, :per], meta_far[0, per:], rows)
    owners = jnp.stack(
        [
            lax.dynamic_index_in_dim(prefix_piece, me_req ^ k, 0, keepdims=False)
            for k in range(half)
        ]
    ) // split_count
    blocks = rows // BLOCK
    stacked_heads = w_query.shape[1] // head_size

    def by_block(values):
        return jnp.tile(values.reshape(blocks, 1, BLOCK), (1, 1, stacked_heads))

    def flags_of(tenants):
        hit = tenants.reshape(blocks, BLOCK, 1) == owners[None, None, :]
        return jnp.max(hit.astype(jnp.int32), axis=1)

    row_ids = jnp.arange(rows, dtype=jnp.int32)
    cosine, sine = rope_tables((PLEN + offset).astype(jnp.float32), head_size)

    query, own_key, own_value = qkv_call(
        place, stream, attn_gain, w_query, w_keyval, cosine, sine, q_gain, k_gain
    )
    query_far = swap(query, "req", half)
    part_0 = send_part(0, query)
    out_far, _ = attention_call(
        query_far, by_block(tenant_far), flags_of(tenant_far), owners, pieces, None
    )
    back = swap(out_far, "req", half)
    out_near, lse_near = attention_call(
        query,
        by_block(tenant),
        flags_of(tenant),
        owners,
        pieces,
        (own_key, own_value, by_block(row_ids - offset)),
    )
    out_near, part_0 = lax.optimization_barrier((out_near, part_0))
    kept, sent = project_call(place, out_near, lse_near, back, w_out, parts)

    def over_cores(kept, sent):
        return kept.astype(F32) + swap(sent, "mlp", 1).astype(F32)

    part_1 = send_part(1, kept)
    summed = over_cores(kept, sent)
    x_bits = [b // 2 for b in bits_of(parts) if b > 1]
    for bit in x_bits:
        got = swap(summed.astype(BF), "mlp", 2 * bit)
        order = [i ^ bit for i in range(parts // 2)]
        summed = summed.astype(BF).astype(F32) + jnp.stack([got[i] for i in order]).astype(F32)
    residual = jnp.stack(stream[0::2]).astype(F32)
    mid = (residual + summed).astype(BF)
    mid_other = swap(mid, "mlp", 1)

    kept, sent = swiglu_call(place, mid, mid_other, mlp_gain, w_gate, w_up, w_down)
    summed = over_cores(kept, sent)
    for bit in x_bits:
        got = swap(summed[bit:].astype(BF), "mlp", 2 * bit)
        summed = summed[:bit] + got.astype(F32)
    out_share = (mid[0].astype(F32) + summed[0]).astype(BF)

    out_share, part_1 = lax.optimization_barrier((out_share, part_1))

    spread = out_share[None]
    for bit in [b for b in bits_of(groups) if b > 1]:
        got = swap(spread, "req", bit)
        count = spread.shape[0]
        spread = (
            jnp.stack([spread, got], axis=0) if count == 1 else jnp.stack([spread, got], axis=1)
        ).reshape(2 * count, rows, width)
    part_2 = send_part(2, spread)
    part_3 = send_part(3, spread)
    top_rows, low_rows = spread[:, : rows // 2], spread[:, rows // 2 :]

    def add_y(values, axis):
        return jnp.stack([values, swap(values, "req", 1)], axis=axis)

    def add_x(values, axis):
        values = jnp.expand_dims(values, axis)
        for bit in x_bits[::-1]:
            values = jnp.concatenate([values, swap(values, "mlp", 2 * bit)], axis=axis)
        return values

    top_rows = add_x(add_y(top_rows, 0), 0)
    low_rows = add_y(add_x(low_rows, 0), 0)
    quads = [
        (top_rows, "xyz"),
        (swap(top_rows, "mlp", 1), "xyz"),
        (low_rows, "yxz"),
        (swap(low_rows, "mlp", 1), "yxz"),
    ]

    codes = jnp.stack([block[w_head.shape[0] :].reshape(-1)[: 2 * rows] for block in part_0])
    codes = codes.astype(F32).astype(jnp.int32)
    wanted = (codes[:, :rows] * 256 + codes[:, rows:]).reshape(groups * rows, 1)
    stats = None
    for first, group_of in ((0, [part_0, part_1, part_2]), (3, [part_3])):
        found = head_call(
            place, quads, final_gain, wanted, group_of, w_head.shape[0], first * cut, span
        )[:, :3]
        stats = found if stats is None else merge_stats(stats, found)

    spread_stats = lax.all_to_all(stats, "req", 0, 0, tiled=True)
    top = jnp.max(spread_stats[:, 0], axis=0)
    total = jnp.sum(spread_stats[:, 1] * jnp.exp(spread_stats[:, 0] - top[None]), axis=0)
    stats = jnp.stack([top, total, jnp.sum(spread_stats[:, 2], axis=0)])
    for bit in bits_of(parts)[::-1]:
        stats = merge_stats(stats, swap(stats, "mlp", bit))
    logprob = stats[2] - stats[0] - jnp.log(stats[1])
    return (out_share, logprob)


def solution(mesh):
    in_specs = (
        P("req", "mlp"),
        P(),
        P(),
        P(),
        P(),
        P(),
        P(None, "mlp"),
        P(None, "mlp"),
        P("mlp", None),
        P(None, "mlp"),
        P(None, "mlp"),
        P("mlp", None),
        P("req", "mlp"),
        P("req"),
        P("req", None),
        P("req", None),
        P(),
        P("req", None, "mlp"),
    )
    out_specs = (P("req", "mlp"), P("req"))
    return jax.shard_map(body, mesh=mesh, in_specs=in_specs, out_specs=out_specs, check_vma=False)
```

```python
import functools
import math

import jax
import jax.numpy as jnp
from jax import lax
from jax.experimental import pallas as pl
from jax.experimental.pallas import tpu as pltpu
from jax.sharding import PartitionSpec as P

TENANTS = 4
PLEN = 4096

EPS = 1e-05
LOG_THETA = math.log(1000000.0)
NEG = -1e30
BF = jnp.bfloat16
F32 = jnp.float32
LANES = 128
BLOCK = 64
KEYS = 1024
MIB = 1 << 20


def params(mib, **more):
    return pltpu.CompilerParams(vmem_limit_bytes=mib * MIB, **more)


def swap(values, axis, bit):
    size = lax.axis_size(axis)
    return lax.ppermute(values, axis, [(i, i ^ bit) for i in range(size)])


def after(values, *events):
    return lax.optimization_barrier((values, *events))[0]


def bits_of(size):
    found = []
    while size > 1:
        size //= 2
        found.append(size)
    return found


def row_layout(lengths, tenants, count):
    ends = jnp.cumsum(lengths)
    row_ids = jnp.arange(count, dtype=jnp.int32)
    request = jnp.sum((row_ids[:, None] >= ends[None, :]).astype(jnp.int32), axis=1)
    onehot = (request[:, None] == jnp.arange(lengths.shape[0], dtype=jnp.int32)[None, :]).astype(
        jnp.int32
    )
    starts = ends - lengths
    offset = row_ids - jnp.sum(onehot * starts[None, :], axis=1)
    tenant = jnp.sum(onehot * tenants[None, :], axis=1)
    return (request, offset, tenant)


def rope_tables(position, size):
    half = size // 2
    freq = jnp.exp(jnp.arange(half, dtype=jnp.float32) * (-2.0 * LOG_THETA / size))
    angle = position[:, None] * freq[None, :]
    cosine, sine = jnp.cos(angle), jnp.sin(angle)
    wide = LANES // size
    return (
        jnp.tile(jnp.concatenate([cosine, cosine], axis=1), (1, wide)),
        jnp.tile(jnp.concatenate([-sine, sine], axis=1), (1, wide)),
    )


def lane_ids(shape):
    return lax.broadcasted_iota(jnp.int32, shape, len(shape) - 1)


def qkv_kernel(place, *refs, width, pieces, scale):
    stream = refs[:pieces]
    gain, wq, wkv, cosine, sine, q_gain, k_gain, q_out, key_out, value_out = refs[pieces:]
    me = place[0]
    model = width * pieces
    loaded = [part[...].astype(F32) for part in stream]
    squares = sum(jnp.sum(part * part, axis=-1, keepdims=True) for part in loaded)
    factor = lax.rsqrt(squares / model + EPS)
    query = None
    keyval = None
    for j in range(pieces):
        quarter = me ^ j
        normed = (loaded[j] * factor * gain[pl.ds(quarter, 1), :]).astype(BF)
        rows = pl.ds(pl.multiple_of(quarter * width, width), width)
        q_part = jnp.dot(normed, wq[rows, :], preferred_element_type=F32)
        kv_part = jnp.dot(normed, wkv[rows, :], preferred_element_type=F32)
        query = q_part if query is None else query + q_part
        keyval = kv_part if keyval is None else keyval + kv_part
    lane = lane_ids((query.shape[0], LANES))
    low = lane < 64
    first = (lane % 64) < 32
    cos_t, sin_t = cosine[...], sine[...]

    def roped(tile, factor_of, head_gain):
        value = tile * factor_of * head_gain
        turned = jnp.where(
            first, pltpu.roll(value, LANES - 32, 1), pltpu.roll(value, 32, 1)
        )
        return value * cos_t + turned * sin_t

    for t in range(query.shape[1] // LANES):
        tile = query[:, t * LANES : (t + 1) * LANES]
        square = tile * tile
        one = jnp.sum(jnp.where(low, square, 0.0), axis=-1, keepdims=True)
        two = jnp.sum(jnp.where(low, 0.0, square), axis=-1, keepdims=True)
        factor_of = lax.rsqrt(jnp.where(low, one, two) / 64.0 + EPS)
        result = roped(tile, factor_of, q_gain[...]).astype(BF)
        q_out[:, t * LANES : (t + 1) * LANES] = (result.astype(F32) * scale).astype(BF)
    heads = keyval.shape[1] // LANES
    keys, values = [], []
    for t in range(heads):
        tile = keyval[:, t * LANES : (t + 1) * LANES]
        one = jnp.sum(jnp.where(low, tile * tile, 0.0), axis=-1, keepdims=True)
        factor_of = lax.rsqrt(one / 64.0 + EPS)
        keys.append(roped(tile, factor_of, k_gain[...]))
        values.append(tile)
    for t in range(0, heads, 2):
        wide = slice(t * 64, min(t + 2, heads) * 64)
        key, value = keys[t], pltpu.roll(values[t], 64, 1)
        if t + 1 < heads:
            key = jnp.where(low, key, pltpu.roll(keys[t + 1], 64, 1))
            value = jnp.where(low, value, values[t + 1])
        count = wide.stop - wide.start
        key_out[:, wide] = key[:, :count].astype(BF)
        value_out[wide, :] = jnp.transpose(value)[:count].astype(BF)


def qkv_call(place, stream, gain, wq, wkv, cosine, sine, q_gain, k_gain):
    pieces = len(stream)
    rows, width = stream[0].shape
    head = q_gain.shape[0]
    twice = LANES // head
    kernel = functools.partial(qkv_kernel, width=width, pieces=pieces, scale=head**-0.5)
    whole = pl.BlockSpec(memory_space=pltpu.VMEM)
    return pl.pallas_call(
        kernel,
        out_shape=(
            jax.ShapeDtypeStruct((rows, wq.shape[1]), BF),
            jax.ShapeDtypeStruct((rows, wkv.shape[1] // 2), BF),
            jax.ShapeDtypeStruct((wkv.shape[1] // 2, rows), BF),
        ),
        in_specs=[pl.BlockSpec(memory_space=pltpu.SMEM)] + [whole] * (pieces + 7),
        out_specs=(whole, whole, whole),
        compiler_params=params(24),
        cost_estimate=pl.CostEstimate(
            flops=2 * rows * width * pieces * (wq.shape[1] + wkv.shape[1]),
            bytes_accessed=2 * (wq.size + wkv.size + rows * width * pieces),
            transcendentals=0,
        ),
        name="qkv",
    )(
        place,
        *stream,
        gain.reshape(pieces, width),
        wq,
        wkv,
        cosine,
        sine,
        jnp.tile(q_gain, twice).reshape(1, LANES),
        jnp.tile(k_gain, twice).reshape(1, LANES),
    )


def split_kernel(kv, key_out, value_out, *, heads):
    low = lane_ids((kv.shape[0], LANES)) < 64
    for t in range(0, heads, 2):
        wide = slice(t * 64, min(t + 2, heads) * 64)
        count = wide.stop - wide.start
        first = kv[:, t * LANES : (t + 1) * LANES].astype(F32)
        key, value = first, pltpu.roll(first, 64, 1)
        if t + 1 < heads:
            second = kv[:, (t + 1) * LANES : (t + 2) * LANES].astype(F32)
            key = jnp.where(low, key, pltpu.roll(second, 64, 1))
            value = jnp.where(low, value, second)
        key_out[:, wide] = key[:, :count].astype(BF)
        value_out[wide, :] = jnp.transpose(value)[:count].astype(BF)


def split_call(kv):
    slab, wide = kv.shape
    rows = 256
    return pl.pallas_call(
        functools.partial(split_kernel, heads=wide // LANES),
        out_shape=(
            jax.ShapeDtypeStruct((slab, wide // 2), BF),
            jax.ShapeDtypeStruct((wide // 2, slab), BF),
        ),
        grid=(slab // rows,),
        in_specs=[pl.BlockSpec((rows, wide), lambda i: (i, 0))],
        out_specs=(
            pl.BlockSpec((rows, wide // 2), lambda i: (i, 0)),
            pl.BlockSpec((wide // 2, rows), lambda i: (0, i)),
        ),
        compiler_params=params(16),
        cost_estimate=pl.CostEstimate(flops=0, bytes_accessed=4 * kv.size, transcendentals=0),
        name="split",
    )(kv)


def attention_kernel(flags, owners, *refs, places, heads, group, own, slab):
    pieces = len(places)
    q_ref, tenant_ref, kv_refs, rest = refs[0], refs[1], refs[2 : 2 + 2 * pieces], refs[2 + 2 * pieces :]
    if own:
        own_key, own_value, begin_ref = rest[:3]
        rest = rest[3:]
    out, lse_out, qp, best, total, accum = rest
    block = pl.program_id(0)
    count = heads * group
    wide = heads * 64
    low = lane_ids((BLOCK, LANES)) < 64

    for i in range(count):
        tile = q_ref[:, (i // 2) * LANES : (i // 2 + 1) * LANES].astype(F32)
        place = (i // group) % 2
        if i % 2 != place:
            tile = pltpu.roll(tile, 64, 1)
        tile = jnp.where(low if place == 0 else ~low, tile, 0.0).astype(BF)
        rows = slice(i * BLOCK, (i + 1) * BLOCK)
        for t in range(0, wide, LANES):
            here = min(LANES, wide - t)
            mine = t // LANES == i // group // 2
            qp[rows, t : t + here] = tile[:, :here] if mine else jnp.zeros((BLOCK, here), BF)

    tenants = tenant_ref[0]

    def attend(keys, values, span, mask=None):
        found = None
        for c in range(0, span, min(KEYS, span)):
            part = slice(c, c + min(KEYS, span))
            score = lax.dot_general(
                keys[part, :], qp[...], (((1,), (1,)), ((), ())), preferred_element_type=F32
            )
            if mask is not None:
                score = jnp.where(mask, score, NEG)
            top = jnp.max(score, axis=0, keepdims=True)
            if found is not None:
                top = jnp.maximum(top, found[0])
            weight = jnp.exp(score - top)
            if mask is not None:
                weight = jnp.where(mask, weight, 0.0)
            summed = jnp.sum(weight, axis=0, keepdims=True)
            value = jnp.dot(values[:, part], weight.astype(BF), preferred_element_type=F32)
            if found is not None:
                keep = jnp.exp(found[0] - top)
                summed = found[1] * keep + summed
                value = found[2] * keep + value
            found = (top, summed, value)
        return found

    if own:
        span = own_key.shape[0]
        key_id = lax.broadcasted_iota(jnp.int32, (span, count * BLOCK), 0)
        row_id = block * BLOCK + lane_ids((1, count * BLOCK)) % BLOCK
        seen = (key_id <= row_id) & (key_id >= begin_ref[0])
        best[...], total[...], accum[...] = attend(own_key, own_value, span, seen)
    else:
        best[...] = jnp.full(best.shape, NEG, F32)
        total[...] = jnp.zeros(total.shape, F32)
        accum[...] = jnp.zeros(accum.shape, F32)

    for j in range(pieces):

        @pl.when(flags[block, places[j]] > 0)
        def _(j=j):
            top, summed, value = attend(kv_refs[2 * j], kv_refs[2 * j + 1], slab)
            ok = tenants == owners[places[j]]
            old = best[...]
            new = jnp.where(ok, jnp.maximum(old, top), old)
            keep = jnp.where(ok, jnp.exp(old - new), 1.0)
            add = jnp.where(ok, jnp.exp(jnp.where(ok, top - new, 0.0)), 0.0)
            best[...] = new
            total[...] = total[...] * keep + summed * add
            accum[...] = accum[...] * keep + value * add

    row_total = total[...]
    some = row_total > 0.0
    safe = jnp.where(some, row_total, 1.0)
    lse = jnp.where(some, best[...] + jnp.log(safe), NEG)
    inverse = 1.0 / safe
    lane = lane_ids((1, count * BLOCK))
    result = accum[:64, :]
    for h in range(1, heads):
        result = jnp.where(lane < h * group * BLOCK, result, accum[h * 64 : (h + 1) * 64, :])
    result = result * inverse
    if own:
        out[0] = result
        lse_out[0] = lse
    else:
        high = lse.astype(BF).astype(F32)
        middle = (lse - high).astype(BF).astype(F32)
        last = (lse - high - middle).astype(BF).astype(F32)
        line = lax.broadcasted_iota(jnp.int32, (16, count * BLOCK), 0)
        packed = jnp.where(
            line == 0, high, jnp.where(line == 1, middle, jnp.where(line == 2, last, 0.0))
        )
        out[0, :64, :] = result.astype(BF)
        out[0, 64:, :] = packed.astype(BF)
        lse_out[0] = lse


def attention_call(query, tenant, flags, owners, pieces, places, own_part, name):
    rows, width = query.shape
    pieces = [pieces[place] for place in places]
    slab, wide = pieces[0][0].shape
    own = own_part is not None
    heads = wide // 64
    group = width // 64 // heads
    stack = heads * group * BLOCK
    blocks = rows // BLOCK
    full = lambda array: pl.BlockSpec(array.shape, lambda b, *_: (0, 0))
    lanes = pl.BlockSpec((1, 1, stack), lambda b, *_: (b, 0, 0))
    operands = [query, tenant] + [array for piece in pieces for array in piece]
    in_specs = [pl.BlockSpec((BLOCK, width), lambda b, *_: (b, 0)), lanes]
    in_specs += [full(array) for piece in pieces for array in piece]
    if own:
        own_key, own_value, begin = own_part
        operands += [own_key, own_value, begin]
        in_specs += [full(own_key), full(own_value), lanes]
    depth = 64 if own else 80
    kernel = functools.partial(
        attention_kernel, places=places, heads=heads, group=group, own=own, slab=slab
    )
    return pl.pallas_call(
        kernel,
        out_shape=(
            jax.ShapeDtypeStruct((blocks, depth, stack), F32 if own else BF),
            jax.ShapeDtypeStruct((blocks, 1, stack), F32),
        ),
        grid_spec=pltpu.PrefetchScalarGridSpec(
            num_scalar_prefetch=2,
            grid=(blocks,),
            in_specs=in_specs,
            out_specs=(pl.BlockSpec((1, depth, stack), lambda b, *_: (b, 0, 0)), lanes),
            scratch_shapes=[
                pltpu.VMEM((stack, wide), BF),
                pltpu.VMEM((1, stack), F32),
                pltpu.VMEM((1, stack), F32),
                pltpu.VMEM((wide, stack), F32),
            ],
        ),
        compiler_params=params(60),
        cost_estimate=pl.CostEstimate(
            flops=4 * rows * group * slab * wide * 4,
            bytes_accessed=4 * slab * wide * len(pieces),
            transcendentals=rows * group * heads * slab,
        ),
        name=name,
    )(flags, owners, *operands)


def project_kernel(
    place, one, lse_one, two, three, w_out, kept, sent, attended, *, count, width, pieces
):
    me = place[0]
    for b in range(one.shape[0]):
        logs = [lse_one[b]]
        for other in (two, three):
            extra = other[b, 64:, :].astype(F32)
            logs.append(extra[0:1] + extra[1:2] + extra[2:3])
        top = functools.reduce(jnp.maximum, logs)
        shares = [jnp.exp(value - top) for value in logs]
        inverse = 1.0 / sum(shares)
        merged = (
            one[b] * (shares[0] * inverse)
            + two[b, :64, :].astype(F32) * (shares[1] * inverse)
            + three[b, :64, :].astype(F32) * (shares[2] * inverse)
        )
        rows = jnp.transpose(jnp.concatenate([merged, jnp.zeros_like(merged)], axis=0))
        for t in range(count // 2):
            left = rows[2 * t * BLOCK : (2 * t + 1) * BLOCK]
            right = rows[(2 * t + 1) * BLOCK : (2 * t + 2) * BLOCK]
            attended[b * BLOCK : (b + 1) * BLOCK, t * LANES : (t + 1) * LANES] = (
                left + pltpu.roll(right, 64, 1)
            ).astype(BF)
    for j in range(pieces):
        columns = pl.ds(pl.multiple_of((me ^ j) * width, width), width)
        part = jnp.dot(attended[...], w_out[:, columns], preferred_element_type=F32)
        (sent if j % 2 else kept)[j // 2] = part.astype(BF)


def project_call(place, one, lse_one, two, three, w_out, pieces):
    rows = one.shape[0] * BLOCK
    model = w_out.shape[1]
    width = model // pieces
    whole = pl.BlockSpec(memory_space=pltpu.VMEM)
    half = jax.ShapeDtypeStruct((pieces // 2, rows, width), BF)
    kernel = functools.partial(
        project_kernel, count=w_out.shape[0] // 64, width=width, pieces=pieces
    )
    return pl.pallas_call(
        kernel,
        out_shape=(half, half),
        in_specs=[pl.BlockSpec(memory_space=pltpu.SMEM)] + [whole] * 5,
        out_specs=(whole, whole),
        scratch_shapes=[pltpu.VMEM((rows, w_out.shape[0]), BF)],
        compiler_params=params(24),
        cost_estimate=pl.CostEstimate(
            flops=2 * rows * w_out.size, bytes_accessed=2 * w_out.size, transcendentals=0
        ),
        name="project",
    )(place, one, lse_one, two, three, w_out)


def swiglu_kernel(
    place, ours, theirs, gain, w_gate, w_up, w_down, kept, sent, normed, accum, *, pieces, width
):
    step = pl.program_id(0)
    me = place[0]

    @pl.when(step == 0)
    def _():
        loaded = [
            (theirs if j % 2 else ours)[j // 2].astype(F32) for j in range(pieces)
        ]
        squares = sum(jnp.sum(part * part, axis=-1, keepdims=True) for part in loaded)
        factor = lax.rsqrt(squares / (pieces * width) + EPS)
        for j in range(pieces):
            quarter = me ^ j
            columns = pl.ds(pl.multiple_of(quarter * width, width), width)
            normed[:, columns] = (loaded[j] * factor * gain[pl.ds(quarter, 1), :]).astype(BF)
        accum[...] = jnp.zeros_like(accum)

    gate = jnp.dot(normed[...], w_gate[...], preferred_element_type=F32)
    upper = jnp.dot(normed[...], w_up[...], preferred_element_type=F32)
    inner = (gate / (1.0 + jnp.exp(-gate)) * upper).astype(BF)
    accum[...] += jnp.dot(inner, w_down[...], preferred_element_type=F32)

    @pl.when(step == pl.num_programs(0) - 1)
    def _():
        for j in range(pieces):
            columns = pl.ds(pl.multiple_of((me ^ j) * width, width), width)
            (sent if j % 2 else kept)[j // 2] = accum[:, columns].astype(BF)


def swiglu_call(place, ours, theirs, gain, w_gate, w_up, w_down):
    half_pieces, rows, width = ours.shape
    pieces = 2 * half_pieces
    model, units = w_gate.shape
    tile = 256
    whole = pl.BlockSpec((half_pieces, rows, width), lambda s, *_: (0, 0, 0))
    half = jax.ShapeDtypeStruct((half_pieces, rows, width), BF)
    kernel = functools.partial(swiglu_kernel, pieces=pieces, width=width)
    return pl.pallas_call(
        kernel,
        out_shape=(half, half),
        grid_spec=pltpu.PrefetchScalarGridSpec(
            num_scalar_prefetch=1,
            grid=(units // tile,),
            in_specs=[
                whole,
                whole,
                pl.BlockSpec((pieces, width), lambda s, *_: (0, 0)),
                pl.BlockSpec((model, tile), lambda s, *_: (0, s)),
                pl.BlockSpec((model, tile), lambda s, *_: (0, s)),
                pl.BlockSpec((tile, model), lambda s, *_: (s, 0)),
            ],
            out_specs=(whole, whole),
            scratch_shapes=[
                pltpu.VMEM((rows, model), BF),
                pltpu.VMEM((rows, model), F32),
            ],
        ),
        compiler_params=params(60),
        cost_estimate=pl.CostEstimate(
            flops=6 * rows * model * units,
            bytes_accessed=6 * model * units,
            transcendentals=rows * units,
        ),
        name="swiglu",
    )(place, ours, theirs, gain.reshape(pieces, width), w_gate, w_up, w_down)


def head_kernel(
    place, *refs, count, locate, depth, offset, span, width, pieces, blocks, widths, code_widths
):
    hidden = refs[:count]
    w_refs = refs[count : count + blocks * len(widths)]
    code_refs = refs[count + blocks * len(widths) : count + blocks * (len(widths) + 1)]
    out, w_full, tile, codes, raw, factors, tops, w_sems, tile_sems, code_sems = refs[
        count + blocks * (len(widths) + 1) :
    ]
    me_req, me_mlp = place[1], place[0]
    rows = tile.shape[1]
    half_rows = rows // 2
    model = tile.shape[2]
    columns_here = w_full.shape[1]

    def fetch(z, y):
        copies = []
        for part in range(2):
            for j in range(pieces):
                index, where = locate(part, j // 2, y, j % 2)
                source = hidden[index]
                for position in where:
                    source = source.at[position if position is not None else z]
                copies.append(
                    pltpu.make_async_copy(
                        source,
                        tile.at[
                            y,
                            pl.ds(part * half_rows, half_rows),
                            pl.ds(pl.multiple_of((me_mlp ^ j) * width, width), width),
                        ],
                        tile_sems.at[y, part * pieces + j],
                    )
                )
        return copies

    w_copies = [
        pltpu.make_async_copy(
            w_refs[n].at[:depth, :],
            w_full.at[
                pl.ds(pl.multiple_of((me_req ^ (n % blocks)) * depth, depth), depth),
                pl.ds(sum(widths[: n // blocks]), widths[n // blocks]),
            ],
            w_sems.at[n],
        )
        for n in range(blocks * len(widths))
    ]
    code_copies = [
        pltpu.make_async_copy(code_refs[k].at[depth:, :], codes.at[k], code_sems.at[k])
        for k in range(blocks)
    ]
    for copy in fetch(0, 0) + code_copies + w_copies:
        copy.start()
    for copy in code_copies + w_copies:
        copy.wait()

    lane = lane_ids((rows, LANES))
    base = me_mlp * (span * blocks) + me_req * span + offset
    step_cols = math.gcd(columns_here, 256)
    lanes_of = lambda values, c: values[:, c * LANES : (c + 1) * LANES]

    def wanted_of(here):
        lines = codes[here].astype(F32)
        flat = jnp.concatenate(
            [lines[l : l + 1] for l in range(-(-2 * rows // code_widths))], axis=1
        )
        wanted = (flat[:, :rows] * 256.0 + flat[:, rows : 2 * rows]).astype(jnp.int32)
        return jnp.transpose(jnp.broadcast_to(wanted, (LANES, rows))) - base - lane

    def stage(new, old, place_old):
        if old is not None:
            factor = factors[old]
            best = tops[old] * factor
            total = jnp.zeros((rows, LANES), F32)
            picked = jnp.zeros((rows, LANES), F32)
            wanted = wanted_of(place_old)
        if new is not None:
            squares = jnp.zeros((rows, LANES), F32)
            top = jnp.full((rows, LANES), NEG, F32)
        steps = columns_here // step_cols
        per_step = -(-(model // LANES) // steps)
        for c in range(steps):
            part = slice(c * step_cols, (c + 1) * step_cols)
            if new is not None:
                logits = jnp.dot(tile[new], w_full[:, part], preferred_element_type=F32)
                raw[new, :, part] = logits
                for t in range(step_cols // LANES):
                    top = jnp.maximum(top, lanes_of(logits, t))
                for t in range(c * per_step, min((c + 1) * per_step, model // LANES)):
                    value = tile[new, :, t * LANES : (t + 1) * LANES].astype(F32)
                    squares = squares + value * value
            if old is not None:
                for t in range(c * step_cols // LANES, (c + 1) * step_cols // LANES):
                    value = raw[old, :, t * LANES : (t + 1) * LANES] * factor
                    total = total + jnp.exp(value - best)
                    picked = jnp.where(wanted == t * LANES, value, picked)
        if new is not None:
            tops[new] = top
            scale = lax.rsqrt(jnp.sum(squares, axis=-1, keepdims=True) / model + EPS)
            factors[new] = jnp.broadcast_to(scale, (rows, LANES))
        if old is not None:
            best = jnp.transpose(best)
            highest = jnp.max(best, axis=0, keepdims=True)
            summed = jnp.sum(jnp.transpose(total) * jnp.exp(best - highest), axis=0, keepdims=True)
            chosen = jnp.sum(jnp.transpose(picked), axis=0, keepdims=True)
            line = lax.broadcasted_iota(jnp.int32, (8, rows), 0)
            joined = jnp.where(line == 0, highest, jnp.where(line == 1, summed, chosen))
            out[pl.ds(place_old ^ me_req, 1)] = joined[None]

    depth_z = blocks // 2

    def begin(z, y):
        for copy in fetch(z, y):
            copy.start()

    def finish(z, y):
        for copy in fetch(z, y):
            copy.wait()

    begin(0, 1)
    finish(0, 0)
    stage(0, None, None)

    def pair(z, carry):
        begin(z + 1, 0)
        finish(z, 1)
        stage(1, 0, 2 * z)
        begin(z + 1, 1)
        finish(z + 1, 0)
        stage(0, 1, 2 * z + 1)
        return carry

    lax.fori_loop(0, depth_z - 1, pair, 0)
    last = depth_z - 1
    finish(last, 1)
    stage(1, 0, 2 * last)
    stage(None, 1, 2 * last + 1)


def head_call(place, hidden, locate, w_parts, codes, depth, offset, span):
    blocks = len(codes)
    widths = [part[0].shape[1] for part in w_parts]
    columns = sum(widths)
    half_rows, width = hidden[0].shape[-2:]
    model = depth * blocks
    pieces = model // width
    rows = 2 * half_rows
    code_widths = codes[0].shape[1]
    kernel = functools.partial(
        head_kernel,
        count=len(hidden),
        locate=locate,
        depth=depth,
        offset=offset,
        span=span,
        width=width,
        pieces=pieces,
        blocks=blocks,
        widths=widths,
        code_widths=code_widths,
    )
    operands = list(hidden) + sum(w_parts, []) + list(codes)
    return pl.pallas_call(
        kernel,
        out_shape=jax.ShapeDtypeStruct((blocks, 8, rows), F32),
        in_specs=[pl.BlockSpec(memory_space=pltpu.SMEM)]
        + [pl.BlockSpec(memory_space=pl.ANY)] * len(operands),
        out_specs=pl.BlockSpec(memory_space=pltpu.VMEM),
        scratch_shapes=[
            pltpu.VMEM((model, columns), BF),
            pltpu.VMEM((2, rows, model), BF),
            pltpu.VMEM((blocks, 16, code_widths), BF),
            pltpu.VMEM((2, rows, columns), F32),
            pltpu.VMEM((2, rows, LANES), F32),
            pltpu.VMEM((2, rows, LANES), F32),
            pltpu.SemaphoreType.DMA((blocks * len(widths),)),
            pltpu.SemaphoreType.DMA((2, 2 * pieces)),
            pltpu.SemaphoreType.DMA((blocks,)),
        ],
        compiler_params=params(60),
        cost_estimate=pl.CostEstimate(
            flops=2 * rows * blocks * model * columns,
            bytes_accessed=2 * model * columns + 2 * rows * blocks * model,
            transcendentals=rows * blocks * columns,
        ),
        name="head",
    )(place, *operands)


def merge_stats(one, two):
    top = jnp.maximum(one[..., 0, :], two[..., 0, :])
    total = one[..., 1, :] * jnp.exp(one[..., 0, :] - top) + two[..., 1, :] * jnp.exp(
        two[..., 0, :] - top
    )
    return jnp.stack([top, total, one[..., 2, :] + two[..., 2, :]], axis=-2)


def body(
    tokens,
    attn_gain,
    mlp_gain,
    final_gain,
    q_gain,
    k_gain,
    w_query,
    w_keyval,
    w_out,
    w_gate,
    w_up,
    w_down,
    w_head,
    targets,
    req_lengths,
    req_tenant,
    prefix_piece,
    prefix_kv,
):
    rows, width = tokens.shape
    groups = lax.axis_size("req")
    parts = lax.axis_size("mlp")
    half = groups // 2
    me_req = lax.axis_index("req")
    me_mlp = lax.axis_index("mlp")
    place = jnp.stack([me_mlp, me_req]).astype(jnp.int32)
    split_count = groups // TENANTS
    head_size = q_gain.shape[0]

    meta_far = swap(jnp.concatenate([req_lengths, req_tenant], axis=1), "req", half)
    per = req_lengths.shape[1]

    pieces = [split_call(prefix_kv[0])]

    stream = [tokens]
    for bit in [b for b in bits_of(parts) if b > 1][::-1]:
        got = swap(jnp.concatenate(stream, axis=1), "mlp", bit)
        stream = stream + [got[:, i * width : (i + 1) * width] for i in range(len(stream))]
    stream, req_lengths, req_tenant, meta_far, prefix_piece = lax.optimization_barrier(
        (stream, req_lengths, req_tenant, meta_far, prefix_piece)
    )
    pieces, w_head, final_gain, targets = lax.optimization_barrier(
        (pieces, w_head, final_gain, targets)
    )
    got = swap(jnp.concatenate(stream, axis=1), "mlp", 1)
    stream = [
        part
        for i, mine in enumerate(stream)
        for part in (mine, got[:, i * width : (i + 1) * width])
    ]

    span = w_head.shape[1] // groups
    quarter = span // 4
    cuts = [(0, 2 * quarter), (2 * quarter, quarter), (3 * quarter, quarter)]
    coded = jnp.concatenate([targets >> 8, targets & 255]).astype(F32).astype(BF)
    coded = coded.reshape(-1, cuts[0][1]) if 2 * rows >= cuts[0][1] else jnp.pad(
        coded, (0, cuts[0][1] - 2 * rows)
    ).reshape(1, -1)
    extra = jnp.pad(coded, ((0, 16 - coded.shape[0]), (0, 0)))

    row_gain = lax.dynamic_slice_in_dim(final_gain, me_req * w_head.shape[0], w_head.shape[0], 0)
    row_gain = row_gain[:, None]

    def head_part(part, k, matrix):
        start, size = cuts[part]
        block = lax.dynamic_slice_in_dim(matrix, (me_req ^ k) * span + start, size, 1)
        block = (block.astype(F32) * row_gain).astype(BF)
        return jnp.concatenate([block, extra], axis=0) if part == 0 else block

    across = groups // 4
    inner = (me_req // across == 1) | (me_req // across == 2)
    head_in = {}
    head_out = {}

    def far(part, place):
        first = half + place * (half // 4)
        return [(part, k) for k in range(first, first + half // 4)]

    def near(part, place):
        return [(part, k) for k in range(1, half) if (k - 1) % 3 == place]

    def send(units, event, where=None):
        blocks = after([head_out[unit] for unit in units], event)
        sent = {}
        for unit, block in zip(units, blocks):
            pairs = [
                (i, i ^ unit[1])
                for i in range(groups)
                if where is None or (i // across in (1, 2)) == (where == "inner")
            ]
            sent[unit] = (where, lax.ppermute(block, "req", pairs))
        return sent

    def arrive(sent, event):
        event, blocks = lax.optimization_barrier(
            (event, {unit: block for unit, (_, block) in sent.items()})
        )
        got = {unit: (sent[unit][0], blocks[unit]) for unit in sent}
        for unit, (where, block) in got.items():
            if unit in head_in:
                block = jnp.where(inner == (where == "inner"), block, head_in[unit])
            head_in[unit] = block
        return event

    far_rest = [k for _, k in far(0, 2) if k != half + half // 2]
    early = [(part, half + half // 2) for part in range(3)]
    head_out.update({unit: head_part(*unit, w_head) for unit in early})
    sent_start = send(early, tokens, "inner")

    request, offset, tenant = row_layout(req_lengths[0], req_tenant[0], rows)
    _, _, tenant_far = row_layout(meta_far[0, :per], meta_far[0, per:], rows)
    owners = jnp.stack(
        [
            lax.dynamic_index_in_dim(prefix_piece, me_req ^ k, 0, keepdims=False)
            for k in range(half)
        ]
    ) // split_count
    blocks = rows // BLOCK
    stacked_heads = w_query.shape[1] // head_size

    def by_block(values):
        return jnp.tile(values.reshape(blocks, 1, BLOCK), (1, 1, stacked_heads))

    def flags_of(tenants):
        hit = tenants.reshape(blocks, BLOCK, 1) == owners[None, None, :]
        return jnp.max(hit.astype(jnp.int32), axis=1)

    row_ids = jnp.arange(rows, dtype=jnp.int32)
    cosine, sine = rope_tables((PLEN + offset).astype(jnp.float32), head_size)

    near_rows = (flags_of(tenant), by_block(tenant), by_block(row_ids - offset))
    far_rows = (flags_of(tenant_far), by_block(tenant_far))
    stream, owners, near_rows, far_rows, cosine, sine = lax.optimization_barrier(
        (stream, owners, near_rows, far_rows, cosine, sine)
    )
    query, own_key, own_value = qkv_call(
        place, stream, attn_gain, w_query, w_keyval, cosine, sine, q_gain, k_gain
    )
    for k in range(1, half):
        if k & (k - 1) == 0:
            pieces.append(tuple(swap(array, "req", k) for array in pieces[0]))
        else:
            pieces.append(None)
    direct = [k for k in range(half) if pieces[k] is not None]
    passed = [k for k in range(half) if pieces[k] is None]
    arrived = [pieces[k] for k in direct]
    arrived, query = lax.optimization_barrier((arrived, query))
    for k, piece in zip(direct, arrived):
        pieces[k] = piece
    for k in passed:
        least, most = k & -k, 1 << (k.bit_length() - 1)
        pieces[k] = (
            swap(pieces[k ^ least][0], "req", least), swap(pieces[k ^ most][1], "req", most)
        )
    query_far = swap(query, "req", half)
    out_near, lse_near = attention_call(
        query,
        near_rows[1],
        near_rows[0],
        owners,
        pieces,
        direct,
        (own_key, own_value, near_rows[2]),
        "attention_near",
    )
    query_far, out_near = lax.optimization_barrier((query_far, out_near))
    query_far = arrive(sent_start, query_far)
    w_rest = after(w_head, query_far)
    for part in range(len(cuts)):
        head_in[part, 0] = head_part(part, 0, w_rest)
        for k in range(1, groups):
            if (part, k) not in head_out:
                head_out[part, k] = head_part(part, k, w_rest)

    sent_one = send(far(0, 1) + near(0, 0), query_far)
    out_far, _ = attention_call(
        query_far, far_rows[1], far_rows[0], owners, pieces, range(half), None, "attention_far"
    )
    out_far = arrive(sent_one, out_far)
    back = swap(out_far, "req", half)
    sent_one = send(far(1, 0) + near(0, 1), out_far)
    query = after(query, out_far)
    out_rest, _ = attention_call(
        query, near_rows[1], near_rows[0], owners, pieces, passed, None, "attention_rest"
    )
    back, out_rest = arrive(sent_one, (back, out_rest))
    kept, sent = project_call(place, out_near, lse_near, back, out_rest, w_out, parts)

    def over_cores(kept, sent):
        return kept.astype(F32) + swap(sent, "mlp", 1).astype(F32)

    sent_one = send(far(0, 0) + near(0, 2), kept)
    summed = over_cores(kept, sent)
    x_bits = [b // 2 for b in bits_of(parts) if b > 1]
    for bit in x_bits:
        got = swap(summed.astype(BF), "mlp", 2 * bit)
        order = [i ^ bit for i in range(parts // 2)]
        summed = summed.astype(BF).astype(F32) + jnp.stack([got[i] for i in order]).astype(F32)
    residual = jnp.stack(stream[0::2]).astype(F32)
    mid = (residual + summed).astype(BF)
    mid = arrive(sent_one, mid)
    mid_other = swap(mid, "mlp", 1)

    sent_one = {**send(far(1, 1) + near(1, 0), mid), **send(far(0, 3), mid, "outer")}
    kept, sent = arrive(
        sent_one, swiglu_call(place, mid, mid_other, mlp_gain, w_gate, w_up, w_down)
    )
    sent_one = {**send(near(1, 1), kept), **send(far(1, 3) + far(2, 3), kept, "inner")}
    summed = over_cores(kept, sent)
    for bit in x_bits:
        got = swap(summed[bit:].astype(BF), "mlp", 2 * bit)
        summed = summed[:bit] + got.astype(F32)
    out_share = (mid[0].astype(F32) + summed[0]).astype(BF)

    out_share = arrive(sent_one, out_share)

    spread = out_share[None]
    for bit in [b for b in bits_of(groups) if b > 1]:
        last = bit == 2
        if last:
            sent_one = send(far(0, 3), spread, "inner")
        got = swap(spread, "req", bit)
        count = spread.shape[0]
        spread = (
            jnp.stack([spread, got], axis=0) if count == 1 else jnp.stack([spread, got], axis=1)
        ).reshape(2 * count, rows, width)
        if last:
            spread = arrive(sent_one, spread)
    middle = half + half // 2
    sent_one = send([(1, middle), (2, middle)] + far(1, 3), spread, "outer")
    top_rows, low_rows = spread[:, : rows // 2], spread[:, rows // 2 :]

    x_count = parts // 2

    def add_x(values, bits):
        for bit in bits:
            values = jnp.concatenate([values, swap(values, "mlp", 2 * bit)], axis=0)
        return values

    top_rows = jnp.stack([top_rows, swap(top_rows, "req", 1)])[None]
    low_rows = add_x(low_rows[None], x_bits[::-1])
    top_rows, low_rows = arrive(sent_one, (top_rows, low_rows))
    sent_one = {
        **send(near(1, 2) + far(2, 0), top_rows),
        **send([(0, half + half // 2)], top_rows, "outer"),
    }
    top_rows = add_x(top_rows, x_bits[::-1][:-1])
    top_more = swap(top_rows, "mlp", 2 * x_bits[0])
    low_more = swap(low_rows, "req", 1)
    others = [(part, k) for part in (0, 1, 2) for k in far_rest]
    sent_one.update(send(others, top_rows))
    top_more, low_more = arrive(sent_one, (top_more, low_more))
    sent_last = {
        **send(far(2, 1), top_more),
        **send(far(2, 3), top_more, "outer"),
        **send(near(2, 0) + near(2, 1) + near(2, 2), top_more),
    }
    hidden = [top_rows, top_more, low_rows, low_more]
    hidden = hidden + [swap(values, "mlp", 1) for values in hidden]
    split_at = x_count // 2

    def locate(part, x, y, core):
        if part == 0:
            return (4 * core + x // split_at, (x % split_at, y, None))
        return (4 * core + 2 + y, (x, None))

    depth = w_head.shape[0]
    codes = [head_in[0, k] for k in range(groups)]

    def head_of(parts_of):
        blocks = [[head_in[part, k] for k in range(groups)] for part in parts_of]
        return head_call(
            place, hidden, locate, blocks, codes, depth, cuts[parts_of[0]][0], span
        )[:, :3]

    stats = arrive(sent_last, head_of([0, 1]))
    stats = merge_stats(stats, head_of([2]))

    spread_stats = lax.all_to_all(stats, "req", 0, 0, tiled=True)
    top = jnp.max(spread_stats[:, 0], axis=0)
    total = jnp.sum(spread_stats[:, 1] * jnp.exp(spread_stats[:, 0] - top[None]), axis=0)
    stats = jnp.stack([top, total, jnp.sum(spread_stats[:, 2], axis=0)])
    for bit in bits_of(parts)[::-1]:
        stats = merge_stats(stats, swap(stats, "mlp", bit))
    logprob = stats[2] - stats[0] - jnp.log(stats[1])
    return (out_share, logprob)


def solution(mesh):
    in_specs = (
        P("req", "mlp"),
        P(),
        P(),
        P(),
        P(),
        P(),
        P(None, "mlp"),
        P(None, "mlp"),
        P("mlp", None),
        P(None, "mlp"),
        P(None, "mlp"),
        P("mlp", None),
        P("req", "mlp"),
        P("req"),
        P("req", None),
        P("req", None),
        P(),
        P("req", None, "mlp"),
    )
    out_specs = (P("req", "mlp"), P("req"))
    return jax.shard_map(body, mesh=mesh, in_specs=in_specs, out_specs=out_specs, check_vma=False)
```

```python
import functools
import math

import jax
import jax.numpy as jnp
from jax import lax
from jax.experimental import pallas as pl
from jax.experimental.pallas import tpu as pltpu
from jax.sharding import PartitionSpec as P

TENANTS = 4
PLEN = 4096

EPS = 1e-05
LOG_THETA = math.log(1000000.0)
NEG = -1e30
BF = jnp.bfloat16
F32 = jnp.float32
LANES = 128
BLOCK = 64
KEYS = 1024
MIB = 1 << 20


def params(mib, **more):
    return pltpu.CompilerParams(vmem_limit_bytes=mib * MIB, **more)


def swap(values, axis, bit):
    size = lax.axis_size(axis)
    return lax.ppermute(values, axis, [(i, i ^ bit) for i in range(size)])


def after(values, *events):
    return lax.optimization_barrier((values, *events))[0]


def bits_of(size):
    found = []
    while size > 1:
        size //= 2
        found.append(size)
    return found


def row_layout(lengths, tenants, count):
    ends = jnp.cumsum(lengths)
    row_ids = jnp.arange(count, dtype=jnp.int32)
    request = jnp.sum((row_ids[:, None] >= ends[None, :]).astype(jnp.int32), axis=1)
    onehot = (request[:, None] == jnp.arange(lengths.shape[0], dtype=jnp.int32)[None, :]).astype(
        jnp.int32
    )
    starts = ends - lengths
    offset = row_ids - jnp.sum(onehot * starts[None, :], axis=1)
    tenant = jnp.sum(onehot * tenants[None, :], axis=1)
    return (request, offset, tenant)


def rope_tables(position, size):
    half = size // 2
    freq = jnp.exp(jnp.arange(half, dtype=jnp.float32) * (-2.0 * LOG_THETA / size))
    angle = position[:, None] * freq[None, :]
    cosine, sine = jnp.cos(angle), jnp.sin(angle)
    wide = LANES // size
    return (
        jnp.tile(jnp.concatenate([cosine, cosine], axis=1), (1, wide)),
        jnp.tile(jnp.concatenate([-sine, sine], axis=1), (1, wide)),
    )


def lane_ids(shape):
    return lax.broadcasted_iota(jnp.int32, shape, len(shape) - 1)


def qkv_kernel(place, *refs, width, pieces, scale):
    stream = refs[:pieces]
    gain, wq, wkv, cosine, sine, q_gain, k_gain, q_out, key_out, value_out = refs[pieces:]
    me = place[0]
    model = width * pieces
    loaded = [part[...].astype(F32) for part in stream]
    squares = sum(jnp.sum(part * part, axis=-1, keepdims=True) for part in loaded)
    factor = lax.rsqrt(squares / model + EPS)
    query = None
    keyval = None
    for j in range(pieces):
        quarter = me ^ j
        normed = (loaded[j] * factor * gain[pl.ds(quarter, 1), :]).astype(BF)
        rows = pl.ds(pl.multiple_of(quarter * width, width), width)
        q_part = jnp.dot(normed, wq[rows, :], preferred_element_type=F32)
        kv_part = jnp.dot(normed, wkv[rows, :], preferred_element_type=F32)
        query = q_part if query is None else query + q_part
        keyval = kv_part if keyval is None else keyval + kv_part
    lane = lane_ids((query.shape[0], LANES))
    low = lane < 64
    first = (lane % 64) < 32
    cos_t, sin_t = cosine[...], sine[...]

    def roped(tile, factor_of, head_gain):
        value = tile * factor_of * head_gain
        turned = jnp.where(
            first, pltpu.roll(value, LANES - 32, 1), pltpu.roll(value, 32, 1)
        )
        return value * cos_t + turned * sin_t

    for t in range(query.shape[1] // LANES):
        tile = query[:, t * LANES : (t + 1) * LANES]
        square = tile * tile
        one = jnp.sum(jnp.where(low, square, 0.0), axis=-1, keepdims=True)
        two = jnp.sum(jnp.where(low, 0.0, square), axis=-1, keepdims=True)
        factor_of = lax.rsqrt(jnp.where(low, one, two) / 64.0 + EPS)
        result = roped(tile, factor_of, q_gain[...]).astype(BF)
        q_out[:, t * LANES : (t + 1) * LANES] = (result.astype(F32) * scale).astype(BF)
    heads = keyval.shape[1] // LANES
    keys, values = [], []
    for t in range(heads):
        tile = keyval[:, t * LANES : (t + 1) * LANES]
        one = jnp.sum(jnp.where(low, tile * tile, 0.0), axis=-1, keepdims=True)
        factor_of = lax.rsqrt(one / 64.0 + EPS)
        keys.append(roped(tile, factor_of, k_gain[...]))
        values.append(tile)
    for t in range(0, heads, 2):
        wide = slice(t * 64, min(t + 2, heads) * 64)
        key, value = keys[t], pltpu.roll(values[t], 64, 1)
        if t + 1 < heads:
            key = jnp.where(low, key, pltpu.roll(keys[t + 1], 64, 1))
            value = jnp.where(low, value, values[t + 1])
        count = wide.stop - wide.start
        key_out[:, wide] = key[:, :count].astype(BF)
        value_out[wide, :] = jnp.transpose(value)[:count].astype(BF)


def qkv_call(place, stream, gain, wq, wkv, cosine, sine, q_gain, k_gain):
    pieces = len(stream)
    rows, width = stream[0].shape
    head = q_gain.shape[0]
    twice = LANES // head
    kernel = functools.partial(qkv_kernel, width=width, pieces=pieces, scale=head**-0.5)
    whole = pl.BlockSpec(memory_space=pltpu.VMEM)
    return pl.pallas_call(
        kernel,
        out_shape=(
            jax.ShapeDtypeStruct((rows, wq.shape[1]), BF),
            jax.ShapeDtypeStruct((rows, wkv.shape[1] // 2), BF),
            jax.ShapeDtypeStruct((wkv.shape[1] // 2, rows), BF),
        ),
        in_specs=[pl.BlockSpec(memory_space=pltpu.SMEM)] + [whole] * (pieces + 7),
        out_specs=(whole, whole, whole),
        compiler_params=params(24),
        cost_estimate=pl.CostEstimate(
            flops=2 * rows * width * pieces * (wq.shape[1] + wkv.shape[1]),
            bytes_accessed=2 * (wq.size + wkv.size + rows * width * pieces),
            transcendentals=0,
        ),
        name="qkv",
    )(
        place,
        *stream,
        gain.reshape(pieces, width),
        wq,
        wkv,
        cosine,
        sine,
        jnp.tile(q_gain, twice).reshape(1, LANES),
        jnp.tile(k_gain, twice).reshape(1, LANES),
    )


def split_kernel(kv, key_out, value_out, *, heads):
    low = lane_ids((kv.shape[0], LANES)) < 64
    for t in range(0, heads, 2):
        wide = slice(t * 64, min(t + 2, heads) * 64)
        count = wide.stop - wide.start
        first = kv[:, t * LANES : (t + 1) * LANES].astype(F32)
        key, value = first, pltpu.roll(first, 64, 1)
        if t + 1 < heads:
            second = kv[:, (t + 1) * LANES : (t + 2) * LANES].astype(F32)
            key = jnp.where(low, key, pltpu.roll(second, 64, 1))
            value = jnp.where(low, value, second)
        key_out[:, wide] = key[:, :count].astype(BF)
        value_out[wide, :] = jnp.transpose(value)[:count].astype(BF)


def split_call(kv):
    slab, wide = kv.shape
    rows = 256
    return pl.pallas_call(
        functools.partial(split_kernel, heads=wide // LANES),
        out_shape=(
            jax.ShapeDtypeStruct((slab, wide // 2), BF),
            jax.ShapeDtypeStruct((wide // 2, slab), BF),
        ),
        grid=(slab // rows,),
        in_specs=[pl.BlockSpec((rows, wide), lambda i: (i, 0))],
        out_specs=(
            pl.BlockSpec((rows, wide // 2), lambda i: (i, 0)),
            pl.BlockSpec((wide // 2, rows), lambda i: (0, i)),
        ),
        compiler_params=params(16),
        cost_estimate=pl.CostEstimate(flops=0, bytes_accessed=4 * kv.size, transcendentals=0),
        name="split",
    )(kv)


def attention_kernel(flags, owners, *refs, places, heads, group, own, slab):
    pieces = len(places)
    q_ref, tenant_ref, kv_refs, rest = refs[0], refs[1], refs[2 : 2 + 2 * pieces], refs[2 + 2 * pieces :]
    if own:
        own_key, own_value, begin_ref = rest[:3]
        rest = rest[3:]
    out, lse_out, qp, best, total, accum = rest
    block = pl.program_id(0)
    count = heads * group
    wide = heads * 64
    low = lane_ids((BLOCK, LANES)) < 64

    for i in range(count):
        tile = q_ref[:, (i // 2) * LANES : (i // 2 + 1) * LANES].astype(F32)
        place = (i // group) % 2
        if i % 2 != place:
            tile = pltpu.roll(tile, 64, 1)
        tile = jnp.where(low if place == 0 else ~low, tile, 0.0).astype(BF)
        rows = slice(i * BLOCK, (i + 1) * BLOCK)
        for t in range(0, wide, LANES):
            here = min(LANES, wide - t)
            mine = t // LANES == i // group // 2
            qp[rows, t : t + here] = tile[:, :here] if mine else jnp.zeros((BLOCK, here), BF)

    tenants = tenant_ref[0]

    def attend(keys, values, span, mask=None):
        found = None
        for c in range(0, span, min(KEYS, span)):
            part = slice(c, c + min(KEYS, span))
            score = lax.dot_general(
                keys[part, :], qp[...], (((1,), (1,)), ((), ())), preferred_element_type=F32
            )
            if mask is not None:
                score = jnp.where(mask, score, NEG)
            top = jnp.max(score, axis=0, keepdims=True)
            if found is not None:
                top = jnp.maximum(top, found[0])
            weight = jnp.exp(score - top)
            if mask is not None:
                weight = jnp.where(mask, weight, 0.0)
            summed = jnp.sum(weight, axis=0, keepdims=True)
            value = jnp.dot(values[:, part], weight.astype(BF), preferred_element_type=F32)
            if found is not None:
                keep = jnp.exp(found[0] - top)
                summed = found[1] * keep + summed
                value = found[2] * keep + value
            found = (top, summed, value)
        return found

    if own:
        span = own_key.shape[0]
        key_id = lax.broadcasted_iota(jnp.int32, (span, count * BLOCK), 0)
        row_id = block * BLOCK + lane_ids((1, count * BLOCK)) % BLOCK
        seen = (key_id <= row_id) & (key_id >= begin_ref[0])
        best[...], total[...], accum[...] = attend(own_key, own_value, span, seen)
    else:
        best[...] = jnp.full(best.shape, NEG, F32)
        total[...] = jnp.zeros(total.shape, F32)
        accum[...] = jnp.zeros(accum.shape, F32)

    for j in range(pieces):

        @pl.when(flags[block, places[j]] > 0)
        def _(j=j):
            top, summed, value = attend(kv_refs[2 * j], kv_refs[2 * j + 1], slab)
            ok = tenants == owners[places[j]]
            old = best[...]
            new = jnp.where(ok, jnp.maximum(old, top), old)
            keep = jnp.where(ok, jnp.exp(old - new), 1.0)
            add = jnp.where(ok, jnp.exp(jnp.where(ok, top - new, 0.0)), 0.0)
            best[...] = new
            total[...] = total[...] * keep + summed * add
            accum[...] = accum[...] * keep + value * add

    row_total = total[...]
    some = row_total > 0.0
    safe = jnp.where(some, row_total, 1.0)
    lse = jnp.where(some, best[...] + jnp.log(safe), NEG)
    inverse = 1.0 / safe
    lane = lane_ids((1, count * BLOCK))
    result = accum[:64, :]
    for h in range(1, heads):
        result = jnp.where(lane < h * group * BLOCK, result, accum[h * 64 : (h + 1) * 64, :])
    result = result * inverse
    if own:
        out[0] = result
        lse_out[0] = lse
    else:
        high = lse.astype(BF).astype(F32)
        middle = (lse - high).astype(BF).astype(F32)
        last = (lse - high - middle).astype(BF).astype(F32)
        line = lax.broadcasted_iota(jnp.int32, (16, count * BLOCK), 0)
        packed = jnp.where(
            line == 0, high, jnp.where(line == 1, middle, jnp.where(line == 2, last, 0.0))
        )
        out[0, :64, :] = result.astype(BF)
        out[0, 64:, :] = packed.astype(BF)
        lse_out[0] = lse


def attention_call(query, tenant, flags, owners, pieces, places, own_part, name):
    rows, width = query.shape
    pieces = [pieces[place] for place in places]
    slab, wide = pieces[0][0].shape
    own = own_part is not None
    heads = wide // 64
    group = width // 64 // heads
    stack = heads * group * BLOCK
    blocks = rows // BLOCK
    full = lambda array: pl.BlockSpec(array.shape, lambda b, *_: (0, 0))
    lanes = pl.BlockSpec((1, 1, stack), lambda b, *_: (b, 0, 0))
    operands = [query, tenant] + [array for piece in pieces for array in piece]
    in_specs = [pl.BlockSpec((BLOCK, width), lambda b, *_: (b, 0)), lanes]
    in_specs += [full(array) for piece in pieces for array in piece]
    if own:
        own_key, own_value, begin = own_part
        operands += [own_key, own_value, begin]
        in_specs += [full(own_key), full(own_value), lanes]
    depth = 64 if own else 80
    kernel = functools.partial(
        attention_kernel, places=places, heads=heads, group=group, own=own, slab=slab
    )
    return pl.pallas_call(
        kernel,
        out_shape=(
            jax.ShapeDtypeStruct((blocks, depth, stack), F32 if own else BF),
            jax.ShapeDtypeStruct((blocks, 1, stack), F32),
        ),
        grid_spec=pltpu.PrefetchScalarGridSpec(
            num_scalar_prefetch=2,
            grid=(blocks,),
            in_specs=in_specs,
            out_specs=(pl.BlockSpec((1, depth, stack), lambda b, *_: (b, 0, 0)), lanes),
            scratch_shapes=[
                pltpu.VMEM((stack, wide), BF),
                pltpu.VMEM((1, stack), F32),
                pltpu.VMEM((1, stack), F32),
                pltpu.VMEM((wide, stack), F32),
            ],
        ),
        compiler_params=params(60),
        cost_estimate=pl.CostEstimate(
            flops=4 * rows * group * slab * wide * 4,
            bytes_accessed=4 * slab * wide * len(pieces),
            transcendentals=rows * group * heads * slab,
        ),
        name=name,
    )(flags, owners, *operands)


def project_kernel(
    place, one, lse_one, two, three, w_out, kept, sent, attended, *, count, width, pieces
):
    me = place[0]
    for b in range(one.shape[0]):
        logs = [lse_one[b]]
        for other in (two, three):
            extra = other[b, 64:, :].astype(F32)
            logs.append(extra[0:1] + extra[1:2] + extra[2:3])
        top = functools.reduce(jnp.maximum, logs)
        shares = [jnp.exp(value - top) for value in logs]
        inverse = 1.0 / sum(shares)
        merged = (
            one[b] * (shares[0] * inverse)
            + two[b, :64, :].astype(F32) * (shares[1] * inverse)
            + three[b, :64, :].astype(F32) * (shares[2] * inverse)
        )
        rows = jnp.transpose(jnp.concatenate([merged, jnp.zeros_like(merged)], axis=0))
        for t in range(count // 2):
            left = rows[2 * t * BLOCK : (2 * t + 1) * BLOCK]
            right = rows[(2 * t + 1) * BLOCK : (2 * t + 2) * BLOCK]
            attended[b * BLOCK : (b + 1) * BLOCK, t * LANES : (t + 1) * LANES] = (
                left + pltpu.roll(right, 64, 1)
            ).astype(BF)
    for j in range(pieces):
        columns = pl.ds(pl.multiple_of((me ^ j) * width, width), width)
        part = jnp.dot(attended[...], w_out[:, columns], preferred_element_type=F32)
        (sent if j % 2 else kept)[j // 2] = part.astype(BF)


def project_call(place, one, lse_one, two, three, w_out, pieces):
    rows = one.shape[0] * BLOCK
    model = w_out.shape[1]
    width = model // pieces
    whole = pl.BlockSpec(memory_space=pltpu.VMEM)
    half = jax.ShapeDtypeStruct((pieces // 2, rows, width), BF)
    kernel = functools.partial(
        project_kernel, count=w_out.shape[0] // 64, width=width, pieces=pieces
    )
    return pl.pallas_call(
        kernel,
        out_shape=(half, half),
        in_specs=[pl.BlockSpec(memory_space=pltpu.SMEM)] + [whole] * 5,
        out_specs=(whole, whole),
        scratch_shapes=[pltpu.VMEM((rows, w_out.shape[0]), BF)],
        compiler_params=params(24),
        cost_estimate=pl.CostEstimate(
            flops=2 * rows * w_out.size, bytes_accessed=2 * w_out.size, transcendentals=0
        ),
        name="project",
    )(place, one, lse_one, two, three, w_out)


def swiglu_kernel(
    place, ours, theirs, gain, w_gate, w_up, w_down, kept, sent, normed, accum, *, pieces, width
):
    step = pl.program_id(0)
    me = place[0]

    @pl.when(step == 0)
    def _():
        loaded = [
            (theirs if j % 2 else ours)[j // 2].astype(F32) for j in range(pieces)
        ]
        squares = sum(jnp.sum(part * part, axis=-1, keepdims=True) for part in loaded)
        factor = lax.rsqrt(squares / (pieces * width) + EPS)
        for j in range(pieces):
            quarter = me ^ j
            columns = pl.ds(pl.multiple_of(quarter * width, width), width)
            normed[:, columns] = (loaded[j] * factor * gain[pl.ds(quarter, 1), :]).astype(BF)
        accum[...] = jnp.zeros_like(accum)

    gate = jnp.dot(normed[...], w_gate[...], preferred_element_type=F32)
    upper = jnp.dot(normed[...], w_up[...], preferred_element_type=F32)
    inner = (gate / (1.0 + jnp.exp(-gate)) * upper).astype(BF)
    accum[...] += jnp.dot(inner, w_down[...], preferred_element_type=F32)

    @pl.when(step == pl.num_programs(0) - 1)
    def _():
        for j in range(pieces):
            columns = pl.ds(pl.multiple_of((me ^ j) * width, width), width)
            (sent if j % 2 else kept)[j // 2] = accum[:, columns].astype(BF)


def swiglu_call(place, ours, theirs, gain, w_gate, w_up, w_down):
    half_pieces, rows, width = ours.shape
    pieces = 2 * half_pieces
    model, units = w_gate.shape
    tile = 256
    whole = pl.BlockSpec((half_pieces, rows, width), lambda s, *_: (0, 0, 0))
    half = jax.ShapeDtypeStruct((half_pieces, rows, width), BF)
    kernel = functools.partial(swiglu_kernel, pieces=pieces, width=width)
    return pl.pallas_call(
        kernel,
        out_shape=(half, half),
        grid_spec=pltpu.PrefetchScalarGridSpec(
            num_scalar_prefetch=1,
            grid=(units // tile,),
            in_specs=[
                whole,
                whole,
                pl.BlockSpec((pieces, width), lambda s, *_: (0, 0)),
                pl.BlockSpec((model, tile), lambda s, *_: (0, s)),
                pl.BlockSpec((model, tile), lambda s, *_: (0, s)),
                pl.BlockSpec((tile, model), lambda s, *_: (s, 0)),
            ],
            out_specs=(whole, whole),
            scratch_shapes=[
                pltpu.VMEM((rows, model), BF),
                pltpu.VMEM((rows, model), F32),
            ],
        ),
        compiler_params=params(60),
        cost_estimate=pl.CostEstimate(
            flops=6 * rows * model * units,
            bytes_accessed=6 * model * units,
            transcendentals=rows * units,
        ),
        name="swiglu",
    )(place, ours, theirs, gain.reshape(pieces, width), w_gate, w_up, w_down)


def head_kernel(
    place, *refs, count, locate, depth, offset, span, width, pieces, blocks, widths, code_widths
):
    hidden = refs[:count]
    w_refs = refs[count : count + blocks * len(widths)]
    code_refs = refs[count + blocks * len(widths) : count + blocks * (len(widths) + 1)]
    out, w_full, tile, codes, raw, factors, tops, w_sems, tile_sems, code_sems = refs[
        count + blocks * (len(widths) + 1) :
    ]
    me_req, me_mlp = place[1], place[0]
    rows = tile.shape[1]
    half_rows = rows // 2
    model = tile.shape[2]
    columns_here = w_full.shape[1]

    def fetch(z, y):
        copies = []
        for part in range(2):
            for j in range(pieces):
                index, where = locate(part, j // 2, y, j % 2)
                source = hidden[index]
                for position in where:
                    source = source.at[position if position is not None else z]
                copies.append(
                    pltpu.make_async_copy(
                        source,
                        tile.at[
                            y,
                            pl.ds(part * half_rows, half_rows),
                            pl.ds(pl.multiple_of((me_mlp ^ j) * width, width), width),
                        ],
                        tile_sems.at[y, part * pieces + j],
                    )
                )
        return copies

    w_copies = [
        pltpu.make_async_copy(
            w_refs[n].at[:depth, :],
            w_full.at[
                pl.ds(pl.multiple_of((me_req ^ (n % blocks)) * depth, depth), depth),
                pl.ds(sum(widths[: n // blocks]), widths[n // blocks]),
            ],
            w_sems.at[n],
        )
        for n in range(blocks * len(widths))
    ]
    code_copies = [
        pltpu.make_async_copy(code_refs[k].at[depth:, :], codes.at[k], code_sems.at[k])
        for k in range(blocks)
    ]
    for copy in fetch(0, 0) + code_copies + w_copies:
        copy.start()
    for copy in code_copies + w_copies:
        copy.wait()

    lane = lane_ids((rows, LANES))
    base = me_mlp * (span * blocks) + me_req * span + offset
    step_cols = math.gcd(columns_here, 256)
    lanes_of = lambda values, c: values[:, c * LANES : (c + 1) * LANES]

    def wanted_of(here):
        lines = codes[here].astype(F32)
        flat = jnp.concatenate(
            [lines[l : l + 1] for l in range(-(-2 * rows // code_widths))], axis=1
        )
        wanted = (flat[:, :rows] * 256.0 + flat[:, rows : 2 * rows]).astype(jnp.int32)
        return jnp.transpose(jnp.broadcast_to(wanted, (LANES, rows))) - base - lane

    def stage(new, old, place_old):
        if old is not None:
            factor = factors[old]
            best = tops[old] * factor
            total = jnp.zeros((rows, LANES), F32)
            picked = jnp.zeros((rows, LANES), F32)
            wanted = wanted_of(place_old)
        if new is not None:
            squares = jnp.zeros((rows, LANES), F32)
            top = jnp.full((rows, LANES), NEG, F32)
        steps = columns_here // step_cols
        per_step = -(-(model // LANES) // steps)
        for c in range(steps):
            part = slice(c * step_cols, (c + 1) * step_cols)
            if new is not None:
                logits = jnp.dot(tile[new], w_full[:, part], preferred_element_type=F32)
                raw[new, :, part] = logits
                for t in range(step_cols // LANES):
                    top = jnp.maximum(top, lanes_of(logits, t))
                for t in range(c * per_step, min((c + 1) * per_step, model // LANES)):
                    value = tile[new, :, t * LANES : (t + 1) * LANES].astype(F32)
                    squares = squares + value * value
            if old is not None:
                for t in range(c * step_cols // LANES, (c + 1) * step_cols // LANES):
                    value = raw[old, :, t * LANES : (t + 1) * LANES] * factor
                    total = total + jnp.exp(value - best)
                    picked = jnp.where(wanted == t * LANES, value, picked)
        if new is not None:
            tops[new] = top
            scale = lax.rsqrt(jnp.sum(squares, axis=-1, keepdims=True) / model + EPS)
            factors[new] = jnp.broadcast_to(scale, (rows, LANES))
        if old is not None:
            best = jnp.transpose(best)
            highest = jnp.max(best, axis=0, keepdims=True)
            summed = jnp.sum(jnp.transpose(total) * jnp.exp(best - highest), axis=0, keepdims=True)
            chosen = jnp.sum(jnp.transpose(picked), axis=0, keepdims=True)
            line = lax.broadcasted_iota(jnp.int32, (8, rows), 0)
            joined = jnp.where(line == 0, highest, jnp.where(line == 1, summed, chosen))
            out[pl.ds(place_old ^ me_req, 1)] = joined[None]

    depth_z = blocks // 2

    def begin(z, y):
        for copy in fetch(z, y):
            copy.start()

    def finish(z, y):
        for copy in fetch(z, y):
            copy.wait()

    begin(0, 1)
    finish(0, 0)
    stage(0, None, None)

    def pair(z, carry):
        begin(z + 1, 0)
        finish(z, 1)
        stage(1, 0, 2 * z)
        begin(z + 1, 1)
        finish(z + 1, 0)
        stage(0, 1, 2 * z + 1)
        return carry

    lax.fori_loop(0, depth_z - 1, pair, 0)
    last = depth_z - 1
    finish(last, 1)
    stage(1, 0, 2 * last)
    stage(None, 1, 2 * last + 1)


def head_call(place, hidden, locate, w_parts, codes, depth, offset, span):
    blocks = len(codes)
    widths = [part[0].shape[1] for part in w_parts]
    columns = sum(widths)
    half_rows, width = hidden[0].shape[-2:]
    model = depth * blocks
    pieces = model // width
    rows = 2 * half_rows
    code_widths = codes[0].shape[1]
    kernel = functools.partial(
        head_kernel,
        count=len(hidden),
        locate=locate,
        depth=depth,
        offset=offset,
        span=span,
        width=width,
        pieces=pieces,
        blocks=blocks,
        widths=widths,
        code_widths=code_widths,
    )
    operands = list(hidden) + sum(w_parts, []) + list(codes)
    return pl.pallas_call(
        kernel,
        out_shape=jax.ShapeDtypeStruct((blocks, 8, rows), F32),
        in_specs=[pl.BlockSpec(memory_space=pltpu.SMEM)]
        + [pl.BlockSpec(memory_space=pl.ANY)] * len(operands),
        out_specs=pl.BlockSpec(memory_space=pltpu.VMEM),
        scratch_shapes=[
            pltpu.VMEM((model, columns), BF),
            pltpu.VMEM((2, rows, model), BF),
            pltpu.VMEM((blocks, 16, code_widths), BF),
            pltpu.VMEM((2, rows, columns), F32),
            pltpu.VMEM((2, rows, LANES), F32),
            pltpu.VMEM((2, rows, LANES), F32),
            pltpu.SemaphoreType.DMA((blocks * len(widths),)),
            pltpu.SemaphoreType.DMA((2, 2 * pieces)),
            pltpu.SemaphoreType.DMA((blocks,)),
        ],
        compiler_params=params(60),
        cost_estimate=pl.CostEstimate(
            flops=2 * rows * blocks * model * columns,
            bytes_accessed=2 * model * columns + 2 * rows * blocks * model,
            transcendentals=rows * blocks * columns,
        ),
        name="head",
    )(place, *operands)


def merge_stats(one, two):
    top = jnp.maximum(one[..., 0, :], two[..., 0, :])
    total = one[..., 1, :] * jnp.exp(one[..., 0, :] - top) + two[..., 1, :] * jnp.exp(
        two[..., 0, :] - top
    )
    return jnp.stack([top, total, one[..., 2, :] + two[..., 2, :]], axis=-2)


def body(
    tokens,
    attn_gain,
    mlp_gain,
    final_gain,
    q_gain,
    k_gain,
    w_query,
    w_keyval,
    w_out,
    w_gate,
    w_up,
    w_down,
    w_head,
    targets,
    req_lengths,
    req_tenant,
    prefix_piece,
    prefix_kv,
):
    rows, width = tokens.shape
    groups = lax.axis_size("req")
    parts = lax.axis_size("mlp")
    half = groups // 2
    me_req = lax.axis_index("req")
    me_mlp = lax.axis_index("mlp")
    place = jnp.stack([me_mlp, me_req]).astype(jnp.int32)
    split_count = groups // TENANTS
    head_size = q_gain.shape[0]

    meta_far = swap(jnp.concatenate([req_lengths, req_tenant], axis=1), "req", half)
    per = req_lengths.shape[1]

    pieces = [split_call(prefix_kv[0])]

    stream = [tokens]
    for bit in [b for b in bits_of(parts) if b > 1][::-1]:
        got = swap(jnp.concatenate(stream, axis=1), "mlp", bit)
        stream = stream + [got[:, i * width : (i + 1) * width] for i in range(len(stream))]
    stream, req_lengths, req_tenant, meta_far, prefix_piece = lax.optimization_barrier(
        (stream, req_lengths, req_tenant, meta_far, prefix_piece)
    )
    pieces, w_head, final_gain, targets = lax.optimization_barrier(
        (pieces, w_head, final_gain, targets)
    )
    got = swap(jnp.concatenate(stream, axis=1), "mlp", 1)
    stream = [
        part
        for i, mine in enumerate(stream)
        for part in (mine, got[:, i * width : (i + 1) * width])
    ]

    span = w_head.shape[1] // groups
    quarter = span // 4
    cuts = [(0, 2 * quarter), (2 * quarter, quarter), (3 * quarter, quarter)]
    coded = jnp.concatenate([targets >> 8, targets & 255]).astype(F32).astype(BF)
    coded = coded.reshape(-1, cuts[0][1]) if 2 * rows >= cuts[0][1] else jnp.pad(
        coded, (0, cuts[0][1] - 2 * rows)
    ).reshape(1, -1)
    extra = jnp.pad(coded, ((0, 16 - coded.shape[0]), (0, 0)))

    row_gain = lax.dynamic_slice_in_dim(final_gain, me_req * w_head.shape[0], w_head.shape[0], 0)
    row_gain = row_gain[:, None]

    def head_part(part, k, matrix):
        start, size = cuts[part]
        block = lax.dynamic_slice_in_dim(matrix, (me_req ^ k) * span + start, size, 1)
        block = (block.astype(F32) * row_gain).astype(BF)
        return jnp.concatenate([block, extra], axis=0) if part == 0 else block

    across = groups // 4
    inner = (me_req // across == 1) | (me_req // across == 2)
    head_in = {}
    head_out = {}

    def far(part, place):
        first = half + place * (half // 4)
        return [(part, k) for k in range(first, first + half // 4)]

    def near(part, place):
        return [(part, k) for k in range(1, half) if (k - 1) % 3 == place]

    def send(units, event, where=None):
        blocks = after([head_out[unit] for unit in units], event)
        sent = {}
        for unit, block in zip(units, blocks):
            pairs = [
                (i, i ^ unit[1])
                for i in range(groups)
                if where is None or (i // across in (1, 2)) == (where == "inner")
            ]
            sent[unit] = (where, lax.ppermute(block, "req", pairs))
        return sent

    def arrive(sent, event):
        event, blocks = lax.optimization_barrier(
            (event, {unit: block for unit, (_, block) in sent.items()})
        )
        got = {unit: (sent[unit][0], blocks[unit]) for unit in sent}
        for unit, (where, block) in got.items():
            if unit in head_in:
                block = jnp.where(inner == (where == "inner"), block, head_in[unit])
            head_in[unit] = block
        return event

    far_rest = [k for _, k in far(0, 2) if k != half + half // 2]
    early = [(part, half + half // 2) for part in range(2)]
    head_out.update({unit: head_part(*unit, w_head) for unit in early})
    sent_start = send(early, tokens, "inner")

    request, offset, tenant = row_layout(req_lengths[0], req_tenant[0], rows)
    _, _, tenant_far = row_layout(meta_far[0, :per], meta_far[0, per:], rows)
    owners = jnp.stack(
        [
            lax.dynamic_index_in_dim(prefix_piece, me_req ^ k, 0, keepdims=False)
            for k in range(half)
        ]
    ) // split_count
    blocks = rows // BLOCK
    stacked_heads = w_query.shape[1] // head_size

    def by_block(values):
        return jnp.tile(values.reshape(blocks, 1, BLOCK), (1, 1, stacked_heads))

    def flags_of(tenants):
        hit = tenants.reshape(blocks, BLOCK, 1) == owners[None, None, :]
        return jnp.max(hit.astype(jnp.int32), axis=1)

    row_ids = jnp.arange(rows, dtype=jnp.int32)
    cosine, sine = rope_tables((PLEN + offset).astype(jnp.float32), head_size)

    near_rows = (flags_of(tenant), by_block(tenant), by_block(row_ids - offset))
    far_rows = (flags_of(tenant_far), by_block(tenant_far))
    stream, owners, near_rows, far_rows, cosine, sine = lax.optimization_barrier(
        (stream, owners, near_rows, far_rows, cosine, sine)
    )
    query, own_key, own_value = qkv_call(
        place, stream, attn_gain, w_query, w_keyval, cosine, sine, q_gain, k_gain
    )
    for k in range(1, half):
        if k & (k - 1) == 0:
            pieces.append(tuple(swap(array, "req", k) for array in pieces[0]))
        else:
            pieces.append(None)
    direct = [k for k in range(half) if pieces[k] is not None]
    passed = [k for k in range(half) if pieces[k] is None]
    arrived = [pieces[k] for k in direct]
    arrived, query = lax.optimization_barrier((arrived, query))
    for k, piece in zip(direct, arrived):
        pieces[k] = piece
    for k in passed:
        least, most = k & -k, 1 << (k.bit_length() - 1)
        pieces[k] = (
            swap(pieces[k ^ least][0], "req", least), swap(pieces[k ^ most][1], "req", most)
        )
    query_far = swap(query, "req", half)
    out_near, lse_near = attention_call(
        query,
        near_rows[1],
        near_rows[0],
        owners,
        pieces,
        direct,
        (own_key, own_value, near_rows[2]),
        "attention_near",
    )
    query_far, out_near = lax.optimization_barrier((query_far, out_near))
    query_far = arrive(sent_start, query_far)
    w_rest = after(w_head, query_far)
    for part in range(len(cuts)):
        head_in[part, 0] = head_part(part, 0, w_rest)
        for k in range(1, groups):
            if (part, k) not in head_out:
                head_out[part, k] = head_part(part, k, w_rest)

    sent_one = send(far(0, 1) + near(0, 0), query_far)
    out_far, _ = attention_call(
        query_far, far_rows[1], far_rows[0], owners, pieces, range(half), None, "attention_far"
    )
    out_far = arrive(sent_one, out_far)
    back = swap(out_far, "req", half)
    sent_one = send(far(1, 0) + near(0, 1), out_far)
    query = after(query, out_far)
    out_rest, _ = attention_call(
        query, near_rows[1], near_rows[0], owners, pieces, passed, None, "attention_rest"
    )
    back, out_rest = arrive(sent_one, (back, out_rest))
    kept, sent = project_call(place, out_near, lse_near, back, out_rest, w_out, parts)

    def over_cores(kept, sent):
        return kept.astype(F32) + swap(sent, "mlp", 1).astype(F32)

    sent_one = send(far(0, 0) + near(0, 2) + near(2, 0), kept)
    summed = over_cores(kept, sent)
    x_bits = [b // 2 for b in bits_of(parts) if b > 1]
    for bit in x_bits:
        got = swap(summed.astype(BF), "mlp", 2 * bit)
        order = [i ^ bit for i in range(parts // 2)]
        summed = summed.astype(BF).astype(F32) + jnp.stack([got[i] for i in order]).astype(F32)
    residual = jnp.stack(stream[0::2]).astype(F32)
    mid = (residual + summed).astype(BF)
    mid = arrive(sent_one, mid)
    mid_other = swap(mid, "mlp", 1)

    sent_one = {**send(far(1, 1) + near(1, 0), mid), **send(far(0, 3), mid, "outer")}
    kept, sent = arrive(
        sent_one, swiglu_call(place, mid, mid_other, mlp_gain, w_gate, w_up, w_down)
    )
    sent_one = {**send(near(1, 1) + near(2, 1), kept), **send(far(1, 3) + far(2, 3), kept, "inner")}
    summed = over_cores(kept, sent)
    for bit in x_bits:
        got = swap(summed[bit:].astype(BF), "mlp", 2 * bit)
        summed = summed[:bit] + got.astype(F32)
    out_share = (mid[0].astype(F32) + summed[0]).astype(BF)

    out_share = arrive(sent_one, out_share)

    spread = out_share[None]
    for bit in [b for b in bits_of(groups) if b > 1]:
        last = bit == 2
        if last:
            sent_one = send(far(0, 3), spread, "inner")
        got = swap(spread, "req", bit)
        count = spread.shape[0]
        spread = (
            jnp.stack([spread, got], axis=0) if count == 1 else jnp.stack([spread, got], axis=1)
        ).reshape(2 * count, rows, width)
        if last:
            spread = arrive(sent_one, spread)
    middle = half + half // 2
    sent_one = send([(1, middle)] + far(1, 3), spread, "outer")
    top_rows, low_rows = spread[:, : rows // 2], spread[:, rows // 2 :]

    x_count = parts // 2

    def add_x(values, bits):
        for bit in bits:
            values = jnp.concatenate([values, swap(values, "mlp", 2 * bit)], axis=0)
        return values

    top_rows = jnp.stack([top_rows, swap(top_rows, "req", 1)])[None]
    low_rows = add_x(low_rows[None], x_bits[::-1])
    top_rows, low_rows = arrive(sent_one, (top_rows, low_rows))
    sent_one = {
        **send(near(1, 2) + far(2, 0), top_rows),
        **send([(0, half + half // 2)], top_rows, "outer"),
    }
    top_rows = add_x(top_rows, x_bits[::-1][:-1])
    top_more = swap(top_rows, "mlp", 2 * x_bits[0])
    low_more = swap(low_rows, "req", 1)
    others = [(part, k) for part in (0, 1, 2) for k in far_rest]
    sent_one.update(send(others, top_rows))
    top_more, low_more = arrive(sent_one, (top_more, low_more))
    sent_last = {
        **send(far(2, 1) + [(2, middle)], top_more),
        **send(far(2, 3), top_more, "outer"),
        **send(near(2, 2), top_more),
    }
    hidden = [top_rows, top_more, low_rows, low_more]
    hidden = hidden + [swap(values, "mlp", 1) for values in hidden]
    split_at = x_count // 2

    def locate(part, x, y, core):
        if part == 0:
            return (4 * core + x // split_at, (x % split_at, y, None))
        return (4 * core + 2 + y, (x, None))

    depth = w_head.shape[0]
    codes = [head_in[0, k] for k in range(groups)]

    def head_of(parts_of):
        blocks = [[head_in[part, k] for k in range(groups)] for part in parts_of]
        return head_call(
            place, hidden, locate, blocks, codes, depth, cuts[parts_of[0]][0], span
        )[:, :3]

    stats = arrive(sent_last, head_of([0, 1]))
    stats = merge_stats(stats, head_of([2]))

    spread_stats = lax.all_to_all(stats, "req", 0, 0, tiled=True)
    top = jnp.max(spread_stats[:, 0], axis=0)
    total = jnp.sum(spread_stats[:, 1] * jnp.exp(spread_stats[:, 0] - top[None]), axis=0)
    stats = jnp.stack([top, total, jnp.sum(spread_stats[:, 2], axis=0)])
    for bit in bits_of(parts)[::-1]:
        stats = merge_stats(stats, swap(stats, "mlp", bit))
    logprob = stats[2] - stats[0] - jnp.log(stats[1])
    return (out_share, logprob)


def solution(mesh):
    in_specs = (
        P("req", "mlp"),
        P(),
        P(),
        P(),
        P(),
        P(),
        P(None, "mlp"),
        P(None, "mlp"),
        P("mlp", None),
        P(None, "mlp"),
        P(None, "mlp"),
        P("mlp", None),
        P("req", "mlp"),
        P("req"),
        P("req", None),
        P("req", None),
        P(),
        P("req", None, "mlp"),
    )
    out_specs = (P("req", "mlp"), P("req"))
    return jax.shard_map(body, mesh=mesh, in_specs=in_specs, out_specs=out_specs, check_vma=False)
```
